128 devices in a mesh: gx: 16 (over x, z_lo, core), gy: 8 (over y, z_hi).
Axes of the slice: x: 4, y: 4, z: 4 (z_hi: 2, z_lo: 2; z = z_hi * 2 + z_lo), core: 2. Of those that a mesh axis runs over, the one named last changes fastest.
Arguments:
- tokens: bfloat16 [512, 8192], P('gy', 'gx'), may hold values from -6 to 6
- out_grad: bfloat16 [512, 8192], P('gy', 'gx'), may hold values from -6 to 6
- gate_weight: bfloat16 [8192, 28672], P('gx', 'gy'), may hold values from -0.0625 to 0.0625
- up_weight: bfloat16 [8192, 28672], P('gx', 'gy'), may hold values from -0.0625 to 0.0625
- down_weight: bfloat16 [28672, 8192], P('gy', 'gx'), may hold values from -0.03125 to 0.03125
Outputs:
- grad_tokens: bfloat16 [512, 8192], P('gy', 'gx')
- grad_gate_weight: bfloat16 [8192, 28672], P('gx', 'gy')
- grad_up_weight: bfloat16 [8192, 28672], P('gx', 'gy')
- grad_down_weight: bfloat16 [28672, 8192], P('gy', 'gx')
The draws below stay inside these ranges and needn't reach their ends.
All inputs are finite; a program needn't handle non-finite values.
Results may differ from the reference program's by a relative error of at most 0.005.
Values may be sent and summed in bfloat16 or wider, within the bound.
No kernel may reach another device: no remote copies, remote signals or barrier semaphores. Data moves between devices by JAX's collectives and lax.ppermute only.
A program may use at most 192 MiB of HBM per device.

```python
import jax
import jax.numpy as jnp
from jax import lax

D = 8192
FF = 28672
TOKENS = 512


def block_levels(rng, shape, split, smallest, high):
    gain, own = 1.0, jax.random.fold_in(rng, 6)
    for axis_at, blocks in split:
        steps = jnp.exp(jax.random.uniform(jax.random.fold_in(own, axis_at), (blocks,), jnp.float32, smallest / len(split), high / len(split)))
        gain = gain * jnp.repeat(steps, shape[axis_at] // blocks).reshape([-1 if axis == axis_at else 1 for axis in range(len(shape))])
    return gain


def bell_draw(key, extent, width, most, pieces=(), dtype=jnp.bfloat16):
    array = width * jax.random.normal(key, extent, jnp.float32)
    if pieces:
        array = array * block_levels(key, extent, pieces, -0.22, 0.18)
    return jnp.clip(array, -most, most).astype(dtype)


def setup_inputs(seed: int = 0) -> dict:
    splits = jax.random.split(jax.random.key(seed), 6)
    return {
        "tokens": bell_draw(splits[0], (TOKENS, D), 1.0, 6.0, ((0, 8), (1, 16))),
        "out_grad": bell_draw(splits[1], (TOKENS, D), 1.0, 6.0, ((0, 8), (1, 16))),
        "gate_weight": bell_draw(splits[2], (D, FF), D ** -0.5, 0.0625, ((0, 16), (1, 8))),
        "up_weight": bell_draw(splits[3], (D, FF), D ** -0.5, 0.0625, ((0, 16), (1, 8))),
        "down_weight": bell_draw(splits[4], (FF, D), FF ** -0.5, 0.03125, ((0, 8), (1, 16))),
    }


def local_grads(gate_sum, upper_sum, back_sum):
    sigmoid_gate = jax.nn.sigmoid(gate_sum)
    silu_gate = gate_sum * sigmoid_gate
    hidden = (silu_gate * upper_sum).astype(jnp.bfloat16)
    grad_gate = (back_sum * upper_sum * sigmoid_gate * (1.0 + gate_sum * (1.0 - sigmoid_gate))).astype(jnp.bfloat16)
    grad_upper = (back_sum * silu_gate).astype(jnp.bfloat16)
    return hidden, grad_gate, grad_upper


def reference(tokens, out_grad, gate_weight, up_weight, down_weight):
    contract_last = (((1,), (1,)), ((), ()))
    contract_first = (((0,), (0,)), ((), ()))
    gate_sum = jnp.dot(tokens, gate_weight, preferred_element_type=jnp.float32)
    upper_sum = jnp.dot(tokens, up_weight, preferred_element_type=jnp.float32)
    back_sum = lax.dot_general(out_grad, down_weight, contract_last, preferred_element_type=jnp.float32)
    hidden, grad_gate, grad_upper = local_grads(gate_sum, upper_sum, back_sum)
    grad_down_weight = lax.dot_general(hidden, out_grad, contract_first, preferred_element_type=jnp.float32).astype(jnp.bfloat16)
    grad_gate_weight = lax.dot_general(tokens, grad_gate, contract_first, preferred_element_type=jnp.float32).astype(jnp.bfloat16)
    grad_up_weight = lax.dot_general(tokens, grad_upper, contract_first, preferred_element_type=jnp.float32).astype(jnp.bfloat16)
    grad_tokens = lax.dot_general(grad_gate, gate_weight, contract_last, preferred_element_type=jnp.float32)
    grad_tokens = grad_tokens + lax.dot_general(grad_upper, up_weight, contract_last, preferred_element_type=jnp.float32)
    return grad_tokens.astype(jnp.bfloat16), grad_gate_weight, grad_up_weight, grad_down_weight
```

```python
import functools

import jax
import jax.numpy as jnp
from jax import lax
from jax.experimental import pallas as pl
from jax.experimental.pallas import tpu as pltpu
from jax.sharding import PartitionSpec as P

BF, F32 = jnp.bfloat16, jnp.float32
BLK = 64
TILE = 256
T_TILES, S_TILES = 3, 4
HALF = (T_TILES + S_TILES) * TILE
VMEM = 40 * 1024 * 1024


def gx_perm(move):
    pairs = []
    for i in range(16):
        x, z, c = move(i // 4, (i // 2) % 2, i % 2)
        pairs.append((i, (x % 4) * 4 + (z % 2) * 2 + c % 2))
    return pairs


CORE = gx_perm(lambda x, z, c: (x, z, c + 1))
XP = gx_perm(lambda x, z, c: (x + 1, z, c))
XM = gx_perm(lambda x, z, c: (x - 1, z, c))
ZS = gx_perm(lambda x, z, c: (x, z + 1, c))


def gy_perm(dy, dh):
    return [(i, ((i // 2 + dy) % 4) * 2 + (i + dh) % 2) for i in range(8)]


def send(a, pairs, axis="gx"):
    return lax.ppermute(a, axis, pairs)


def dot(a, b, ca, cb):
    return lax.dot_general(a, b, (((ca,), (cb,)), ((), ())), preferred_element_type=F32)


def place(pos, r):
    return (((r // 2 - pos[0]) & 3) * 2 + ((r & 1) ^ pos[1])) * BLK


def whole(shape):
    return pl.BlockSpec(shape, lambda i, pos: (0,) * len(shape))


def params():
    return pltpu.CompilerParams(vmem_limit_bytes=VMEM, dimension_semantics=("arbitrary",))


def order_kernel(pos, *refs):
    pieces, (tg, tok_t) = refs[:8], refs[8:]
    for r in range(8):
        tg[pl.ds(pl.multiple_of(place(pos, r), BLK), BLK), :] = pieces[r][...]
    tok_t[...] = tg[:, :512].T


def order(pos, pieces):
    return pl.pallas_call(
        order_kernel,
        grid_spec=pltpu.PrefetchScalarGridSpec(
            num_scalar_prefetch=1,
            grid=(1,),
            in_specs=[whole((BLK, 1024))] * 8,
            out_specs=[whole((512, 1024)), whole((512, 512))],
        ),
        out_shape=[jax.ShapeDtypeStruct((512, 1024), BF), jax.ShapeDtypeStruct((512, 512), BF)],
        compiler_params=params(),
        cost_estimate=pl.CostEstimate(flops=0, bytes_accessed=4 << 20, transcendentals=0),
    )(pos, *pieces)


def sums_kernel(split, pos, tg, tg_sib, gw, uw, dw, gw_sib, uw_sib, dw_sib, *outs):
    for a in range(3):
        if a < 2:
            own, sib = ((gw, gw_sib), (uw, uw_sib))[a]
            total = dot(tg[:, :512], own[...], 1, 0) + dot(tg_sib[:, :512], sib[...], 1, 0)
        else:
            total = dot(tg[:, 512:], dw[...], 1, 1) + dot(tg_sib[:, 512:], dw_sib[...], 1, 1)
        split(a, lambda j: total[j * BLK : (j + 1) * BLK], *outs)


def split_s(a, block, m1p, m1m, m2p, m2m, k1, k3, k0, k01):
    m1p[a] = block(4).astype(BF)
    m1m[a] = block(5).astype(BF)
    m2p[a] = block(3).astype(BF)
    m2m[a] = block(6).astype(BF)
    k1[a] = block(2)
    k3[a] = block(7)
    k0[a] = block(0)
    k01[a] = block(1)


def split_t(a, block, mza, mzb, keep):
    mza[a] = block(5).astype(BF)
    for i, jx in enumerate((1, 3, 0)):
        mzb[i, a] = block(jx * 2 + 1).astype(BF)
    for jx in range(4):
        keep[jx, a] = block(jx * 2)


def sums(pos, tg, tg_sib, weights, weights_sib, split, first, tiles, lead):
    cols, rows = (512, TILE), (TILE, 512)
    own = lambda i, pos: (0, pos[2] * (HALF // TILE) + first + i)
    sib = lambda i, pos: (0, first + i)
    flip = lambda f: (lambda i, pos: f(i, pos)[::-1])
    width = tiles * TILE

    def out_spec(n):
        zeros = (0,) * (n + 2)
        return lambda i, pos: (*zeros, i)

    flops = 2 * 3 * 512 * 1024 * width
    return pl.pallas_call(
        functools.partial(sums_kernel, split),
        grid_spec=pltpu.PrefetchScalarGridSpec(
            num_scalar_prefetch=1,
            grid=(tiles,),
            in_specs=[
                whole((512, 1024)),
                whole((512, 1024)),
                pl.BlockSpec(cols, own),
                pl.BlockSpec(cols, own),
                pl.BlockSpec(rows, flip(own)),
                pl.BlockSpec(cols, sib),
                pl.BlockSpec(cols, sib),
                pl.BlockSpec(rows, flip(sib)),
            ],
            out_specs=[pl.BlockSpec((*n, 3, BLK, TILE), out_spec(len(n))) for n, _ in lead],
        ),
        out_shape=[jax.ShapeDtypeStruct((*n, 3, BLK, width), t) for n, t in lead],
        compiler_params=params(),
        cost_estimate=pl.CostEstimate(flops=flops, bytes_accessed=16 << 20, transcendentals=0),
    )(pos, tg, tg_sib, *weights, *weights_sib)


def input_grads_kernel(first, last, pos, grads, tok_t, gw, uw, *refs):
    if first:
        ggw, guw, *out, acc = refs
    else:
        before, _, _, ggw, guw, *out, acc = refs
    step = pl.program_id(0)
    gate, upper = grads[0], grads[1]
    ggw[...] = dot(tok_t[...], gate, 1, 0).astype(BF)
    guw[...] = dot(tok_t[...], upper, 1, 0).astype(BF)
    term = dot(gate, gw[...], 1, 1) + dot(upper, uw[...], 1, 1)

    @pl.when(step == 0)
    def _():
        acc[...] = term if first else before[...] + term

    @pl.when(step > 0)
    def _():
        acc[...] += term

    @pl.when(step == pl.num_programs(0) - 1)
    def _():
        if not last:
            out[0][...] = acc[...]
        else:
            for r in range(8):
                out[r][...] = acc[pl.ds(pl.multiple_of(place(pos, r), BLK), BLK), :]


def input_grads(pos, grads, tok_t, gw, uw, at, carry, last):
    tiles = grads.shape[-1] // TILE
    first = carry is None
    tile = lambda i, pos: (0, at(pos) + i)
    weight = pl.BlockSpec((512, TILE), tile)
    square = whole((512, 512))
    in_specs = [pl.BlockSpec((2, 512, TILE), lambda i, pos: (0, 0, i)), square, weight, weight]
    if not first:
        in_specs += [square, pl.BlockSpec(memory_space=pl.ANY), pl.BlockSpec(memory_space=pl.ANY)]
    full = jax.ShapeDtypeStruct((512, 2 * HALF), BF)
    if last:
        tail_specs, tail = [whole((BLK, 512))] * 8, [jax.ShapeDtypeStruct((BLK, 512), F32)] * 8
    else:
        tail_specs, tail = [square], [jax.ShapeDtypeStruct((512, 512), F32)]
    outs = pl.pallas_call(
        functools.partial(input_grads_kernel, first, last),
        grid_spec=pltpu.PrefetchScalarGridSpec(
            num_scalar_prefetch=1,
            grid=(tiles,),
            in_specs=in_specs,
            out_specs=[weight, weight, *tail_specs],
            scratch_shapes=[pltpu.VMEM((512, 512), F32)],
        ),
        out_shape=[full, full, *tail],
        input_output_aliases={} if first else {6: 0, 7: 1},
        compiler_params=params(),
        cost_estimate=pl.CostEstimate(
            flops=8 * 512 * 512 * tiles * TILE, bytes_accessed=tiles << 20, transcendentals=0
        ),
    )(pos, grads, tok_t, gw, uw, *([] if first else [carry[2], carry[0], carry[1]]))
    return outs


def down_grad_kernel(pos, hidden, tg, *refs):
    refs[-1][...] = dot(hidden[...], tg[:, 512:], 0, 0).astype(BF)


def down_grad(pos, hidden, tg, at, carry):
    tiles = hidden.shape[-1] // TILE
    rest = [] if carry is None else [carry]
    return pl.pallas_call(
        down_grad_kernel,
        grid_spec=pltpu.PrefetchScalarGridSpec(
            num_scalar_prefetch=1,
            grid=(tiles,),
            in_specs=[pl.BlockSpec((512, TILE), lambda i, pos: (0, i)), whole((512, 1024))]
            + [pl.BlockSpec(memory_space=pl.ANY)] * len(rest),
            out_specs=pl.BlockSpec((TILE, 512), lambda i, pos: (at(pos) + i, 0)),
        ),
        out_shape=jax.ShapeDtypeStruct((2 * HALF, 512), BF),
        input_output_aliases={3: 0} if rest else {},
        compiler_params=params(),
        cost_estimate=pl.CostEstimate(
            flops=2 * 512 * 512 * tiles * TILE, bytes_accessed=3 << 20, transcendentals=0
        ),
    )(pos, hidden, tg, *rest)


def wide(a):
    return a.astype(F32)


def scatter_s(m1p, m1m, m2p, m2m, k1, k3, k0, k01):
    r1p, r1m = send(m1p, XP), send(m1m, XM)
    r2p, r2m = send(m2p, XP), send(m2m, XM)
    r3p = send((k1 + wide(r1p)).astype(BF), XP)
    r3m = send((k3 + wide(r1m)).astype(BF), XM)
    rz = send((k01 + wide(r2p) + wide(r3m)).astype(BF), ZS)
    return k0 + wide(r2m) + wide(r3p) + wide(rz)


def scatter_t(mza, mzb, keep):
    rza, rzb = send(mza, ZS), send(mzb, ZS)
    d2 = (keep[2] + wide(rza)).astype(BF)
    r1p, r1m = send(d2[:, :32], XP), send(d2[:, 32:], XM)
    d1, d3, d0 = keep[1] + wide(rzb[0]), keep[3] + wide(rzb[1]), keep[0] + wide(rzb[2])
    r2p, r2m = send(d1[:, 32:].astype(BF), XP), send(d3[:, :32].astype(BF), XM)
    r3p = send((d1[:, :32] + wide(r1p)).astype(BF), XP)
    r3m = send((d3[:, 32:] + wide(r1m)).astype(BF), XM)
    low = d0[:, :32] + wide(r3p) + wide(r2m)
    high = d0[:, 32:] + wide(r2p) + wide(r3m)
    return jnp.concatenate([low, high], axis=1)


def gather_s(e):
    ez = send(e, ZS)
    g30, g10 = send(e, XP), send(e, XM)
    g31, g11 = send(ez, XP), send(ez, XM)
    g20, g21 = send(g30, XP), send(g11, XM)
    return jnp.concatenate([e, ez, g10, g11, g20, g21, g30, g31], axis=-2)


def gather_t(e):
    h3, h1 = send(e, XP), send(e, XM)
    z0 = send(e, ZS)
    lo, hi = send(h3[..., :32, :], XP), send(h1[..., 32:, :], XM)
    z1, z3 = send(h1, ZS), send(h3, ZS)
    zlo, zhi = send(lo, ZS), send(hi, ZS)
    return jnp.concatenate([e, z0, h1, z1, lo, hi, zlo, zhi, h3, z3], axis=-2)


def local_grads(gate_sum, upper_sum, back_sum):
    sigmoid_gate = jax.nn.sigmoid(gate_sum)
    silu_gate = gate_sum * sigmoid_gate
    hidden = (silu_gate * upper_sum).astype(BF)
    grad_gate = (
        back_sum * upper_sum * sigmoid_gate * (1.0 + gate_sum * (1.0 - sigmoid_gate))
    ).astype(BF)
    grad_upper = (back_sum * silu_gate).astype(BF)
    return hidden, jnp.stack([grad_gate, grad_upper])


def shards(tokens, out_grad, gate_weight, up_weight, down_weight):
    gx = lax.axis_index("gx")
    core = gx % 2
    pos = jnp.stack([gx // 4, (gx // 2) % 2, core]).astype(jnp.int32)
    far = (1 - core) * HALF

    both = jnp.concatenate([tokens, out_grad], axis=1)
    pieces = [both] + [send(both, gy_perm(-(r // 2), r % 2), "gy") for r in range(1, 8)]
    weights = (gate_weight, up_weight, down_weight)
    weights_sib = [
        send(lax.dynamic_slice_in_dim(w, far, HALF, axis), CORE)
        for w, axis in zip(weights, (1, 1, 0))
    ]
    tg, tok_t = order(pos, pieces)
    tg_sib = send(tg, CORE)

    lead_t = [((), BF), ((3,), BF), ((4,), F32)]
    lead_s = [((), BF)] * 4 + [((), F32)] * 4
    parts_t = sums(pos, tg, tg_sib, weights, weights_sib, split_t, 0, T_TILES, lead_t)
    parts_s = sums(pos, tg, tg_sib, weights, weights_sib, split_s, T_TILES, S_TILES, lead_s)
    sum_s = scatter_s(*parts_s)
    sum_t = scatter_t(*parts_t)
    hidden_s, grads_s = local_grads(sum_s[0], sum_s[1], sum_s[2])
    hidden_t, grads_t = local_grads(sum_t[0], sum_t[1], sum_t[2])

    full_s, full_t = gather_s(grads_s), gather_t(grads_t)
    sib_s, sib_t = send(full_s, CORE), send(full_t, CORE)
    hid_s, hid_t = gather_s(hidden_s), gather_t(hidden_t)
    hid_s_sib, hid_t_sib = send(hid_s, CORE), send(hid_t, CORE)

    per_half = HALF // TILE
    own_t = lambda pos: pos[2] * per_half
    own_s = lambda pos: pos[2] * per_half + T_TILES
    far_t = lambda pos: (1 - pos[2]) * per_half
    far_s = lambda pos: (1 - pos[2]) * per_half + T_TILES
    carry = None
    for grads, at in ((full_t, own_t), (full_s, own_s), (sib_t, far_t), (sib_s, far_s)):
        last = grads is sib_s
        carry = input_grads(pos, grads, tok_t, gate_weight, up_weight, at, carry, last)
    ggw, guw, *terms = carry
    total = terms[0]
    for r in range(1, 8):
        total = total + send(terms[r], gy_perm(r // 2, r % 2), "gy")

    gdw = None
    for hidden, at in ((hid_t, own_t), (hid_s, own_s), (hid_t_sib, far_t), (hid_s_sib, far_s)):
        gdw = down_grad(pos, hidden, tg, at, gdw)
    return total.astype(BF), ggw, guw, gdw


def solution(mesh):
    return jax.shard_map(
        shards,
        mesh=mesh,
        in_specs=(P("gy", "gx"), P("gy", "gx"), P("gx", "gy"), P("gx", "gy"), P("gy", "gx")),
        out_specs=(P("gy", "gx"), P("gx", "gy"), P("gx", "gy"), P("gy", "gx")),
        check_vma=False,
    )
```

```python
import functools

import jax
import jax.numpy as jnp
from jax import lax
from jax.experimental import pallas as pl
from jax.experimental.pallas import tpu as pltpu
from jax.sharding import PartitionSpec as P

BF, F32 = jnp.bfloat16, jnp.float32
BLK = 64
TILE = 256
HALF = 7 * TILE
CUTS = (512, 1152)
MID = HALF // 2
TURN = CUTS[0], CUTS[1] - CUTS[0], HALF - CUTS[1]
ORDER = ((2, 1), (2, 0), (1, 1), (3, 1), (1, 0), (3, 0), (0, 1), (0, 0))
PLACES = sum(i << 4 * (2 * jx + jz) for i, (jx, jz) in enumerate(ORDER))


def gx_perm(move):
    pairs = []
    for i in range(16):
        x, z, c = move(i // 4, (i // 2) % 2, i % 2)
        pairs.append((i, (x % 4) * 4 + (z % 2) * 2 + c % 2))
    return pairs


CORE = gx_perm(lambda x, z, c: (x, z, c + 1))
XP = gx_perm(lambda x, z, c: (x + 1, z, c))
XM = gx_perm(lambda x, z, c: (x - 1, z, c))
ZS = gx_perm(lambda x, z, c: (x, z + 1, c))


def send(a, pairs):
    return lax.ppermute(a, "gx", pairs)


def dot(a, b, ca, cb):
    return lax.dot_general(a, b, (((ca,), (cb,)), ((), ())), preferred_element_type=F32)


def place(pos, b):
    chip = ((b // 2 - pos[0]) & 3) * 2 + ((b & 1) ^ pos[1])
    row = ((PLACES >> (4 * chip)) & 7) * BLK
    return pl.ds(pl.multiple_of(row, BLK), BLK)


def whole(shape):
    return pl.BlockSpec(shape, lambda i, pos: (0,) * len(shape))


def params(mib):
    return pltpu.CompilerParams(vmem_limit_bytes=mib << 20, dimension_semantics=("arbitrary",))


def spread_kernel(tokens, out_grad, copies):
    for b in range(8):
        copies[b, :, :512] = tokens[...]
        copies[b, :, 512:] = out_grad[...]


def spread(tokens, out_grad):
    return pl.pallas_call(
        spread_kernel,
        out_shape=jax.ShapeDtypeStruct((8, BLK, 1024), BF),
        compiler_params=pltpu.CompilerParams(vmem_limit_bytes=16 << 20),
        cost_estimate=pl.CostEstimate(flops=0, bytes_accessed=1 << 20, transcendentals=0),
    )(tokens, out_grad)


def order_kernel(pos, blocks, tg, tok_t):
    for b in range(8):
        tg[place(pos, b), :] = blocks[b]
    tok_t[...] = tg[:, :512].T


def order(pos, blocks):
    return pl.pallas_call(
        order_kernel,
        grid_spec=pltpu.PrefetchScalarGridSpec(
            num_scalar_prefetch=1,
            grid=(1,),
            in_specs=[whole((8, BLK, 1024))],
            out_specs=[whole((512, 1024)), whole((512, 512))],
        ),
        out_shape=[jax.ShapeDtypeStruct((512, 1024), BF), jax.ShapeDtypeStruct((512, 512), BF)],
        compiler_params=params(40),
        cost_estimate=pl.CostEstimate(flops=0, bytes_accessed=4 << 20, transcendentals=0),
    )(pos, blocks)


def sums_kernel(part, pos, tg, tg_sib, gw, uw, dw, gw_sib, uw_sib, dw_sib, *outs):
    for a in range(3):
        if a < 2:
            own, sib = ((gw, gw_sib), (uw, uw_sib))[a]
            total = dot(tg[:, :512], own[...], 1, 0) + dot(tg_sib[:, :512], sib[...], 1, 0)
        else:
            total = dot(tg[:, 512:], dw[...], 1, 1) + dot(tg_sib[:, 512:], dw_sib[...], 1, 1)
        blocks = [total[i * BLK : (i + 1) * BLK] for i in range(4)]
        for block, out in zip(blocks[part == 0 :], outs):
            out[a] = block
        if part == 0:
            far, (z, up, down) = blocks[0].astype(BF), outs[3:]
            up_lo = MID - CUTS[0]

            @pl.when(pl.program_id(0) == 0)
            def _():
                z[a] = far[:, : CUTS[0]]
                up[a, :, :up_lo] = far[:, CUTS[0] :]

            @pl.when(pl.program_id(0) == 1)
            def _():
                up[a, :, up_lo:] = far[:, : CUTS[1] - MID]
                down[a] = far[:, CUTS[1] - MID :]


def sums(pos, tg, tg_sib, weights, weights_sib, part):
    tile = MID
    cols, rows = (512, tile), (tile, 512)
    own = lambda i, pos: (0, pos[2] * 2 + i)
    sib = lambda i, pos: (0, i)
    flip = lambda f: (lambda i, pos: f(i, pos)[::-1])
    tokens = pl.BlockSpec((256, 1024), lambda i, pos: (part, 0))
    kept = 3 if part == 0 else 4
    far = [(3, BLK, width) for width in TURN] if part == 0 else []
    return pl.pallas_call(
        functools.partial(sums_kernel, part),
        grid_spec=pltpu.PrefetchScalarGridSpec(
            num_scalar_prefetch=1,
            grid=(2,),
            in_specs=[
                tokens,
                tokens,
                pl.BlockSpec(cols, own),
                pl.BlockSpec(cols, own),
                pl.BlockSpec(rows, flip(own)),
                pl.BlockSpec(cols, sib),
                pl.BlockSpec(cols, sib),
                pl.BlockSpec(rows, flip(sib)),
            ],
            out_specs=[pl.BlockSpec((3, BLK, tile), lambda i, pos: (0, 0, i))] * kept
            + [whole(shape) for shape in far],
        ),
        out_shape=[jax.ShapeDtypeStruct((3, BLK, HALF), F32)] * kept
        + [jax.ShapeDtypeStruct(shape, BF) for shape in far],
        compiler_params=params(40),
        cost_estimate=pl.CostEstimate(
            flops=2 * 3 * 256 * 1024 * HALF, bytes_accessed=20 << 20, transcendentals=0
        ),
    )(pos, tg, tg_sib, *weights, *weights_sib)


def stack(half, grads, near, mids, far):
    up, down, flat = 0, 1, 2
    grads[:, :BLK] = far[...]
    grads[:, 4 * BLK :] = near[...]
    for i, piece in enumerate((down, flat, up) if half else (up, down, flat)):
        grads[:, (i + 1) * BLK : (i + 2) * BLK] = mids[:, piece * BLK : (piece + 1) * BLK]


def part_kernel(half, has_terms, has_weights, carried, last, pos, *refs):
    refs = list(refs)
    near, mids, far = (refs.pop(0) for _ in range(3))
    gw, uw = (refs.pop(0) for _ in range(2)) if has_terms else (None, None)
    before = refs.pop(0) if has_terms and carried else None
    tok_t, tg = (refs.pop(0) for _ in range(2)) if has_weights else (None, None)
    grads = refs.pop()
    acc = refs.pop() if has_terms else None
    stack(half, grads, near, mids, far)
    if has_weights:
        ggw, guw, gdw = refs[-3:]
        ggw[...] = dot(tok_t[...], grads[0], 1, 0).astype(BF)
        guw[...] = dot(tok_t[...], grads[1], 1, 0).astype(BF)
        gdw[...] = dot(grads[2], tg[:, 512:], 0, 0).astype(BF)
    if has_terms:
        out = refs[-4] if has_weights else refs[-1]
        term = dot(grads[0], gw[...], 1, 1) + dot(grads[1], uw[...], 1, 1)
        if carried:
            term += before[...]
        if not last:
            out[...] = term
        else:
            acc[...] = term
            for b in range(8):
                out[b] = acc[place(pos, b), :].astype(BF)


def part(pos, pieces, core, half, terms=None, weights=None, last=False):
    tile = lambda pos: (core ^ pos[2]) * 2 + half
    arrays = 3 if weights else 2
    column = pl.BlockSpec((512, MID), lambda i, pos: (0, tile(pos)))
    row = pl.BlockSpec((MID, 512), lambda i, pos: (tile(pos), 0))
    square = whole((512, 512))
    in_specs = [
        pl.BlockSpec((arrays, r, MID), lambda i, pos: (0, 0, half)) for r in (256, 192, 64)
    ]
    args, out_specs, out_shape, scratch, aliases = [*pieces], [], [], [], {}
    carried = False
    if terms:
        gw, uw, before = terms
        in_specs += [column, column]
        args += [gw, uw]
        carried = before is not None
        if carried:
            in_specs.append(square)
            args.append(before)
        if last:
            out_specs.append(whole((8, BLK, 512)))
            out_shape.append(jax.ShapeDtypeStruct((8, BLK, 512), BF))
        else:
            out_specs.append(square)
            out_shape.append(jax.ShapeDtypeStruct((512, 512), F32))
        scratch.append(pltpu.VMEM((512, 512), F32))
    if weights:
        tok_t, tg, beside = weights
        in_specs += [square, whole((512, 1024))]
        args += [tok_t, tg]
        if beside is not None:
            for k in range(3):
                aliases[len(args) + 1 + k] = len(out_specs) + k
            in_specs += [pl.BlockSpec(memory_space=pl.ANY)] * 3
            args += beside
        out_specs += [column, column, row]
        out_shape += [jax.ShapeDtypeStruct((512, 2 * HALF), BF)] * 2
        out_shape += [jax.ShapeDtypeStruct((2 * HALF, 512), BF)]
    scratch.append(pltpu.VMEM((arrays, 512, MID), BF))
    flops = 2 * 512 * 512 * MID * (2 * bool(terms) + 3 * bool(weights))
    return pl.pallas_call(
        functools.partial(part_kernel, half, bool(terms), bool(weights), carried, last),
        grid_spec=pltpu.PrefetchScalarGridSpec(
            num_scalar_prefetch=1,
            grid=(1,),
            in_specs=in_specs,
            out_specs=out_specs,
            scratch_shapes=scratch,
        ),
        out_shape=out_shape,
        input_output_aliases=aliases,
        compiler_params=params(32),
        cost_estimate=pl.CostEstimate(flops=flops, bytes_accessed=8 << 20, transcendentals=0),
    )(pos, *args)


def wide(a):
    return a.astype(F32)


def lo(a):
    return a[..., :MID]


def hi(a):
    return a[..., MID:]


def join(*parts):
    return jnp.concatenate(parts, axis=-1)


def merge_kernel(p20, p11, p31, rz, rp, rm, down, up, flat):
    z, x = CUTS
    for a in range(3):
        down[a, :, :z] = (p20[a, :, :z] + wide(rz[a])).astype(BF)
        down[a, :, z:MID] = p20[a, :, z:MID].astype(BF)
        down[a, :, MID:x] = p31[a, :, MID:x].astype(BF)
        down[a, :, x:] = (p31[a, :, x:] + wide(rm[a])).astype(BF)
        up[a, :, :z] = p11[a, :, :z].astype(BF)
        up[a, :, z:MID] = (p11[a, :, z:MID] + wide(rp[a, :, : MID - z])).astype(BF)
        up[a, :, MID:] = p20[a, :, MID:].astype(BF)
        flat[a, :, :MID] = p31[a, :, :MID].astype(BF)
        flat[a, :, MID:x] = (p11[a, :, MID:x] + wide(rp[a, :, MID - z :])).astype(BF)
        flat[a, :, x:] = p11[a, :, x:].astype(BF)


def scatter_far(p20, p11, p31, far_z, far_up, far_down):
    return pl.pallas_call(
        merge_kernel,
        out_shape=[jax.ShapeDtypeStruct((3, BLK, HALF), BF)] * 3,
        compiler_params=pltpu.CompilerParams(vmem_limit_bytes=32 << 20),
        cost_estimate=pl.CostEstimate(flops=0, bytes_accessed=6 << 20, transcendentals=0),
    )(p20, p11, p31, send(far_z, ZS), send(far_up, XP), send(far_down, XM))


def scatter_mid(down, up, flat, p10, p30, p01):
    rm, rp, rz = wide(send(down, XM)), wide(send(up, XP)), wide(send(flat, ZS))
    p10 = join(lo(p10), hi(p10) + hi(rp) + hi(rz))
    p30 = join(lo(p30) + lo(rm) + lo(rz), hi(p30))
    p01 = join(lo(p01) + lo(rp), hi(p01) + hi(rm))
    return p10.astype(BF), p30.astype(BF), p01.astype(BF)


def scatter_last(up, down, flat, p00):
    rp, rm, rz = send(up, XP), send(down, XM), send(flat, ZS)
    return p00 + wide(rp) + wide(rm) + wide(rz)


def rows(*blocks):
    return jnp.concatenate(blocks, axis=-2)


def after(*arrays):
    return lax.optimization_barrier(arrays)


def gather(e):
    z, x = CUTS
    g30, g10, g01 = send(e, XP), send(e, XM), send(e, ZS)
    rp = send(join(lo(g30), hi(g01)), XP)
    rm = send(join(lo(g01), hi(g10)), XM)
    rz = send(join(lo(g30), hi(g10)), ZS)
    turn_up = join(rz[..., z:MID], rp[..., MID:x])
    fz, fp, fm = send(rp[..., :z], ZS), send(turn_up, XP), send(rz[..., x:], XM)
    far, near, mids = after(join(fz, fp, fm), rows(g10, g30, g01, e), rows(rp, rm, rz))
    pieces = near, mids, far
    return pieces, [send(piece, CORE) for piece in pieces]


def local_grads(gate_sum, upper_sum, back_sum):
    sigmoid_gate = jax.nn.sigmoid(gate_sum)
    silu_gate = gate_sum * sigmoid_gate
    hidden = (silu_gate * upper_sum).astype(BF)
    grad_gate = (
        back_sum * upper_sum * sigmoid_gate * (1.0 + gate_sum * (1.0 - sigmoid_gate))
    ).astype(BF)
    grad_upper = (back_sum * silu_gate).astype(BF)
    return jnp.stack([grad_gate, grad_upper, hidden])


def shards(tokens, out_grad, gate_weight, up_weight, down_weight):
    gx = lax.axis_index("gx")
    core = gx % 2
    pos = jnp.stack([gx // 4, (gx // 2) % 2, core]).astype(jnp.int32)
    far_half = (1 - core) * HALF

    blocks = lax.all_to_all(spread(tokens, out_grad), "gy", 0, 0, tiled=True)
    weights = (gate_weight, up_weight, down_weight)
    weights_sib = [
        send(lax.dynamic_slice_in_dim(w, far_half, HALF, axis), CORE)
        for w, axis in zip(weights, (1, 1, 0))
    ]
    tg, tok_t = order(pos, blocks)
    tg_sib = send(tg, CORE)

    first = sums(pos, tg, tg_sib, weights, weights_sib, 0)
    p10, p30, p01, p00 = sums(pos, tg, tg_sib, weights, weights_sib, 1)
    mid = scatter_far(*first)
    last = scatter_mid(*mid, p10, p30, p01)
    total = scatter_last(*last, p00)
    own, sib = gather(local_grads(total[0], total[1], total[2]))

    gw, uw = gate_weight, up_weight
    terms, *grads = part(pos, own, 0, 0, (gw, uw, None), (tok_t, tg, None))
    terms, *grads = part(pos, own, 0, 1, (gw, uw, terms), (tok_t, tg, grads))
    (terms,) = part(pos, sib, 1, 0, (gw, uw, terms))
    (terms,) = part(pos, sib, 1, 1, (gw, uw, terms), None, True)
    grad_tokens = jnp.sum(wide(lax.all_to_all(terms, "gy", 0, 0, tiled=True)), axis=0).astype(BF)
    grads = part(pos, sib, 1, 0, None, (tok_t, tg, grads))
    ggw, guw, gdw = part(pos, sib, 1, 1, None, (tok_t, tg, grads))
    return grad_tokens, ggw, guw, gdw


def solution(mesh):
    return jax.shard_map(
        shards,
        mesh=mesh,
        in_specs=(P("gy", "gx"), P("gy", "gx"), P("gx", "gy"), P("gx", "gy"), P("gy", "gx")),
        out_specs=(P("gy", "gx"), P("gx", "gy"), P("gx", "gy"), P("gy", "gx")),
        check_vma=False,
    )
```

```python
import functools

import jax
import jax.numpy as jnp
from jax import lax
from jax.experimental import pallas as pl
from jax.experimental.pallas import tpu as pltpu
from jax.sharding import PartitionSpec as P

BF, F32 = jnp.bfloat16, jnp.float32
BLK = 64
TILE = 256
HALF = 7 * TILE
CUTS = (512, 1152)
MID = HALF // 2
TURN = CUTS[0], CUTS[1] - CUTS[0], HALF - CUTS[1]
ORDER = ((2, 1), (2, 0), (1, 1), (3, 1), (1, 0), (3, 0), (0, 1), (0, 0))
PLACES = sum(i << 4 * (2 * jx + jz) for i, (jx, jz) in enumerate(ORDER))


def gx_perm(move):
    pairs = []
    for i in range(16):
        x, z, c = move(i // 4, (i // 2) % 2, i % 2)
        pairs.append((i, (x % 4) * 4 + (z % 2) * 2 + c % 2))
    return pairs


CORE = gx_perm(lambda x, z, c: (x, z, c + 1))
XP = gx_perm(lambda x, z, c: (x + 1, z, c))
XM = gx_perm(lambda x, z, c: (x - 1, z, c))
ZS = gx_perm(lambda x, z, c: (x, z + 1, c))


def send(a, pairs):
    return lax.ppermute(a, "gx", pairs)


def dot(a, b, ca, cb):
    return lax.dot_general(a, b, (((ca,), (cb,)), ((), ())), preferred_element_type=F32)


def place(pos, b):
    chip = ((b // 2 - pos[0]) & 3) * 2 + ((b & 1) ^ pos[1])
    row = ((PLACES >> (4 * chip)) & 7) * BLK
    return pl.ds(pl.multiple_of(row, BLK), BLK)


def whole(shape):
    return pl.BlockSpec(shape, lambda i, pos: (0,) * len(shape))


def params(mib):
    return pltpu.CompilerParams(vmem_limit_bytes=mib << 20, dimension_semantics=("arbitrary",))


def spread_kernel(tokens, out_grad, copies):
    for b in range(8):
        copies[b, :, :512] = tokens[...]
        copies[b, :, 512:] = out_grad[...]


def spread(tokens, out_grad):
    return pl.pallas_call(
        spread_kernel,
        out_shape=jax.ShapeDtypeStruct((8, BLK, 1024), BF),
        compiler_params=pltpu.CompilerParams(vmem_limit_bytes=58 << 20),
        cost_estimate=pl.CostEstimate(flops=0, bytes_accessed=1 << 20, transcendentals=0),
    )(tokens, out_grad)


def order_kernel(pos, blocks, tg, tok_t):
    for b in range(8):
        tg[place(pos, b), :] = blocks[b]
    tok_t[...] = tg[:, :512].T


def order(pos, blocks):
    return pl.pallas_call(
        order_kernel,
        grid_spec=pltpu.PrefetchScalarGridSpec(
            num_scalar_prefetch=1,
            grid=(1,),
            in_specs=[whole((8, BLK, 1024))],
            out_specs=[whole((512, 1024)), whole((512, 512))],
        ),
        out_shape=[jax.ShapeDtypeStruct((512, 1024), BF), jax.ShapeDtypeStruct((512, 512), BF)],
        compiler_params=params(40),
        cost_estimate=pl.CostEstimate(flops=0, bytes_accessed=4 << 20, transcendentals=0),
    )(pos, blocks)


def sums_kernel(part, pos, tg, tg_sib, gw, uw, dw, gw_sib, uw_sib, dw_sib, *outs):
    for a in range(3):
        if a < 2:
            own, sib = ((gw, gw_sib), (uw, uw_sib))[a]
            total = dot(tg[:, :512], own[...], 1, 0) + dot(tg_sib[:, :512], sib[...], 1, 0)
        else:
            total = dot(tg[:, 512:], dw[...], 1, 1) + dot(tg_sib[:, 512:], dw_sib[...], 1, 1)
        blocks = [total[i * BLK : (i + 1) * BLK] for i in range(4)]
        for block, out in zip(blocks[part == 0 :], outs):
            out[a] = block
        if part == 0:
            far, (z, up, down) = blocks[0].astype(BF), outs[3:]
            up_lo = MID - CUTS[0]

            @pl.when(pl.program_id(0) == 0)
            def _():
                z[a] = far[:, : CUTS[0]]
                up[a, :, :up_lo] = far[:, CUTS[0] :]

            @pl.when(pl.program_id(0) == 1)
            def _():
                up[a, :, up_lo:] = far[:, : CUTS[1] - MID]
                down[a] = far[:, CUTS[1] - MID :]


def sums(pos, tg, tg_sib, weights, weights_sib, part):
    tile = MID
    cols, rows = (512, tile), (tile, 512)
    own = lambda i, pos: (0, pos[2] * 2 + i)
    sib = lambda i, pos: (0, i)
    flip = lambda f: (lambda i, pos: f(i, pos)[::-1])
    tokens = pl.BlockSpec((256, 1024), lambda i, pos: (part, 0))
    kept = 3 if part == 0 else 4
    far = [(3, BLK, width) for width in TURN] if part == 0 else []
    return pl.pallas_call(
        functools.partial(sums_kernel, part),
        grid_spec=pltpu.PrefetchScalarGridSpec(
            num_scalar_prefetch=1,
            grid=(2,),
            in_specs=[
                tokens,
                tokens,
                pl.BlockSpec(cols, own),
                pl.BlockSpec(cols, own),
                pl.BlockSpec(rows, flip(own)),
                pl.BlockSpec(cols, sib),
                pl.BlockSpec(cols, sib),
                pl.BlockSpec(rows, flip(sib)),
            ],
            out_specs=[pl.BlockSpec((3, BLK, tile), lambda i, pos: (0, 0, i))] * kept
            + [whole(shape) for shape in far],
        ),
        out_shape=[jax.ShapeDtypeStruct((3, BLK, HALF), F32)] * kept
        + [jax.ShapeDtypeStruct(shape, BF) for shape in far],
        compiler_params=params(40),
        cost_estimate=pl.CostEstimate(
            flops=2 * 3 * 256 * 1024 * HALF, bytes_accessed=20 << 20, transcendentals=0
        ),
    )(pos, tg, tg_sib, *weights, *weights_sib)


PIECES = [pl.BlockSpec(memory_space=pl.ANY)] * 3
COPIES = 5


def stack(half, grads, near, mids, far, sems):
    arrays = pl.ds(0, grads.shape[0])
    columns = pl.ds(half * MID, MID)
    up, down, flat = 0, 1, 2
    ways = [(far, 0, 0, BLK), (near, 0, 4 * BLK, 4 * BLK)]
    for i, piece in enumerate((down, flat, up) if half else (up, down, flat)):
        ways.append((mids, piece * BLK, (i + 1) * BLK, BLK))
    copies = [
        pltpu.make_async_copy(
            source.at[arrays, pl.ds(at, size), columns], grads.at[:, pl.ds(to, size), :], sems.at[k]
        )
        for k, (source, at, to, size) in enumerate(ways)
    ]
    for copy in copies:
        copy.start()
    return copies


def wait(copies):
    for copy in copies:
        copy.wait()


def part_kernel(half, has_terms, has_weights, carried, last, pos, *refs):
    refs = list(refs)
    near, mids, far = (refs.pop(0) for _ in range(3))
    gw, uw = (refs.pop(0) for _ in range(2)) if has_terms else (None, None)
    before = refs.pop(0) if has_terms and carried else None
    tok_t, tg = (refs.pop(0) for _ in range(2)) if has_weights else (None, None)
    sems, grads = refs.pop(), refs.pop()
    acc = refs.pop() if has_terms else None
    wait(stack(half, grads, near, mids, far, sems))
    if has_weights:
        ggw, guw, gdw = refs[-3:]
        ggw[...] = dot(tok_t[...], grads[0], 1, 0).astype(BF)
        guw[...] = dot(tok_t[...], grads[1], 1, 0).astype(BF)
        gdw[...] = dot(grads[2], tg[:, 512:], 0, 0).astype(BF)
    if has_terms:
        out = refs[-4] if has_weights else refs[-1]
        term = dot(grads[0], gw[...], 1, 1) + dot(grads[1], uw[...], 1, 1)
        if carried:
            term += before[...]
        if not last:
            out[...] = term
        else:
            acc[...] = term
            for b in range(8):
                out[b] = acc[place(pos, b), :].astype(BF)


def part(pos, pieces, core, half, terms=None, weights=None, last=False):
    tile = lambda pos: (core ^ pos[2]) * 2 + half
    arrays = 3 if weights else 2
    column = pl.BlockSpec((512, MID), lambda i, pos: (0, tile(pos)))
    row = pl.BlockSpec((MID, 512), lambda i, pos: (tile(pos), 0))
    square = whole((512, 512))
    in_specs = [*PIECES]
    args, out_specs, out_shape, scratch, aliases = [*pieces], [], [], [], {}
    carried = False
    if terms:
        gw, uw, before = terms
        in_specs += [column, column]
        args += [gw, uw]
        carried = before is not None
        if carried:
            in_specs.append(square)
            args.append(before)
        if last:
            out_specs.append(whole((8, BLK, 512)))
            out_shape.append(jax.ShapeDtypeStruct((8, BLK, 512), BF))
        else:
            out_specs.append(square)
            out_shape.append(jax.ShapeDtypeStruct((512, 512), F32))
        scratch.append(pltpu.VMEM((512, 512), F32))
    if weights:
        tok_t, tg, beside = weights
        in_specs += [square, whole((512, 1024))]
        args += [tok_t, tg]
        if beside is not None:
            for k in range(3):
                aliases[len(args) + 1 + k] = len(out_specs) + k
            in_specs += [pl.BlockSpec(memory_space=pl.ANY)] * 3
            args += beside
        out_specs += [column, column, row]
        out_shape += [jax.ShapeDtypeStruct((512, 2 * HALF), BF)] * 2
        out_shape += [jax.ShapeDtypeStruct((2 * HALF, 512), BF)]
    scratch += [pltpu.VMEM((arrays, 512, MID), BF), pltpu.SemaphoreType.DMA((COPIES,))]
    flops = 2 * 512 * 512 * MID * (2 * bool(terms) + 3 * bool(weights))
    return pl.pallas_call(
        functools.partial(part_kernel, half, bool(terms), bool(weights), carried, last),
        grid_spec=pltpu.PrefetchScalarGridSpec(
            num_scalar_prefetch=1,
            grid=(1,),
            in_specs=in_specs,
            out_specs=out_specs,
            scratch_shapes=scratch,
        ),
        out_shape=out_shape,
        input_output_aliases=aliases,
        compiler_params=params(32 if terms else 48),
        cost_estimate=pl.CostEstimate(flops=flops, bytes_accessed=8 << 20, transcendentals=0),
    )(pos, *args)


def total_kernel(terms, out):
    total = wide(terms[0])
    for b in range(1, 8):
        total += wide(terms[b])
    out[...] = total.astype(BF)


def total_of(terms):
    return pl.pallas_call(
        total_kernel,
        out_shape=jax.ShapeDtypeStruct((BLK, 512), BF),
        compiler_params=pltpu.CompilerParams(vmem_limit_bytes=8 << 20),
        cost_estimate=pl.CostEstimate(flops=1 << 18, bytes_accessed=1 << 19, transcendentals=0),
    )(terms)


def wide(a):
    return a.astype(F32)


def lo(a):
    return a[..., :MID]


def hi(a):
    return a[..., MID:]


def join(*parts):
    return jnp.concatenate(parts, axis=-1)


def merge_kernel(p20, p11, p31, rz, rp, rm, down, up, flat):
    z, x = CUTS
    for a in range(3):
        down[a, :, :z] = (p20[a, :, :z] + wide(rz[a])).astype(BF)
        down[a, :, z:MID] = p20[a, :, z:MID].astype(BF)
        down[a, :, MID:x] = p31[a, :, MID:x].astype(BF)
        down[a, :, x:] = (p31[a, :, x:] + wide(rm[a])).astype(BF)
        up[a, :, :z] = p11[a, :, :z].astype(BF)
        up[a, :, z:MID] = (p11[a, :, z:MID] + wide(rp[a, :, : MID - z])).astype(BF)
        up[a, :, MID:] = p20[a, :, MID:].astype(BF)
        flat[a, :, :MID] = p31[a, :, :MID].astype(BF)
        flat[a, :, MID:x] = (p11[a, :, MID:x] + wide(rp[a, :, MID - z :])).astype(BF)
        flat[a, :, x:] = p11[a, :, x:].astype(BF)


def scatter_far(p20, p11, p31, far_z, far_up, far_down):
    return pl.pallas_call(
        merge_kernel,
        out_shape=[jax.ShapeDtypeStruct((3, BLK, HALF), BF)] * 3,
        compiler_params=pltpu.CompilerParams(vmem_limit_bytes=32 << 20),
        cost_estimate=pl.CostEstimate(flops=0, bytes_accessed=6 << 20, transcendentals=0),
    )(p20, p11, p31, send(far_z, ZS), send(far_up, XP), send(far_down, XM))


def scatter_mid(down, up, flat, p10, p30, p01):
    rm, rp, rz = wide(send(down, XM)), wide(send(up, XP)), wide(send(flat, ZS))
    p10 = join(lo(p10), hi(p10) + hi(rp) + hi(rz))
    p30 = join(lo(p30) + lo(rm) + lo(rz), hi(p30))
    p01 = join(lo(p01) + lo(rp), hi(p01) + hi(rm))
    return p10.astype(BF), p30.astype(BF), p01.astype(BF)


def scatter_last(up, down, flat, p00):
    rp, rm, rz = send(up, XP), send(down, XM), send(flat, ZS)
    return p00 + wide(rp) + wide(rm) + wide(rz)


def rows(*blocks):
    return jnp.concatenate(blocks, axis=-2)


def after(*arrays):
    return lax.optimization_barrier(arrays)


def gather(e):
    z, x = CUTS
    g30, g10, g01 = send(e, XP), send(e, XM), send(e, ZS)
    rp = send(join(lo(g30), hi(g01)), XP)
    rm = send(join(lo(g01), hi(g10)), XM)
    rz = send(join(lo(g30), hi(g10)), ZS)
    rp, rm, rz, near = after(rp, rm, rz, rows(g10, g30, g01, e))
    turn_up = join(rz[..., z:MID], rp[..., MID:x])
    fz, fp, fm = send(rp[..., :z], ZS), send(turn_up, XP), send(rz[..., x:], XM)
    far, mids = after(join(fz, fp, fm), rows(rp, rm, rz))
    pieces = near, mids, far
    return pieces, [send(piece, CORE) for piece in pieces]


def local_grads(gate_sum, upper_sum, back_sum):
    sigmoid_gate = jax.nn.sigmoid(gate_sum)
    silu_gate = gate_sum * sigmoid_gate
    hidden = (silu_gate * upper_sum).astype(BF)
    grad_gate = (
        back_sum * upper_sum * sigmoid_gate * (1.0 + gate_sum * (1.0 - sigmoid_gate))
    ).astype(BF)
    grad_upper = (back_sum * silu_gate).astype(BF)
    return jnp.stack([grad_gate, grad_upper, hidden])


def shards(tokens, out_grad, gate_weight, up_weight, down_weight):
    gx = lax.axis_index("gx")
    core = gx % 2
    pos = jnp.stack([gx // 4, (gx // 2) % 2, core]).astype(jnp.int32)
    far_half = (1 - core) * HALF

    blocks = lax.all_to_all(spread(tokens, out_grad), "gy", 0, 0, tiled=True)
    weights = (gate_weight, up_weight, down_weight)
    weights_sib = [
        send(lax.dynamic_slice_in_dim(w, far_half, HALF, axis), CORE)
        for w, axis in zip(weights, (1, 1, 0))
    ]
    tg, tok_t = order(pos, blocks)
    tg_sib = send(tg, CORE)

    first = sums(pos, tg, tg_sib, weights, weights_sib, 0)
    p10, p30, p01, p00 = sums(pos, tg, tg_sib, weights, weights_sib, 1)
    mid = scatter_far(*first)
    last = scatter_mid(*mid, p10, p30, p01)
    total = scatter_last(*last, p00)
    own, sib = gather(local_grads(total[0], total[1], total[2]))

    gw, uw = gate_weight, up_weight
    terms, *grads = part(pos, own, 0, 0, (gw, uw, None), (tok_t, tg, None))
    terms, *grads = part(pos, own, 0, 1, (gw, uw, terms), (tok_t, tg, grads))
    (terms,) = part(pos, sib, 1, 0, (gw, uw, terms))
    (terms,) = part(pos, sib, 1, 1, (gw, uw, terms), None, True)
    grad_tokens = total_of(lax.all_to_all(terms, "gy", 0, 0, tiled=True))
    grads = part(pos, sib, 1, 0, None, (tok_t, tg, grads))
    ggw, guw, gdw = part(pos, sib, 1, 1, None, (tok_t, tg, grads))
    return grad_tokens, ggw, guw, gdw


def solution(mesh):
    return jax.shard_map(
        shards,
        mesh=mesh,
        in_specs=(P("gy", "gx"), P("gy", "gx"), P("gx", "gy"), P("gx", "gy"), P("gy", "gx")),
        out_specs=(P("gy", "gx"), P("gx", "gy"), P("gx", "gy"), P("gy", "gx")),
        check_vma=False,
    )
```

```python
import functools

import jax
import jax.numpy as jnp
from jax import lax
from jax.experimental import pallas as pl
from jax.experimental.pallas import tpu as pltpu
from jax.sharding import PartitionSpec as P

BF, F32 = jnp.bfloat16, jnp.float32
BLK = 64
TILE = 256
HALF = 7 * TILE
CUTS = (512, 1152)
MID = HALF // 2
TURN = CUTS[0], CUTS[1] - CUTS[0], HALF - CUTS[1]
ORDER = ((2, 1), (2, 0), (1, 1), (3, 1), (1, 0), (3, 0), (0, 1), (0, 0))
PLACES = sum(i << 4 * (2 * jx + jz) for i, (jx, jz) in enumerate(ORDER))


def gx_perm(move):
    pairs = []
    for i in range(16):
        x, z, c = move(i // 4, (i // 2) % 2, i % 2)
        pairs.append((i, (x % 4) * 4 + (z % 2) * 2 + c % 2))
    return pairs


CORE = gx_perm(lambda x, z, c: (x, z, c + 1))
XP = gx_perm(lambda x, z, c: (x + 1, z, c))
XM = gx_perm(lambda x, z, c: (x - 1, z, c))
ZS = gx_perm(lambda x, z, c: (x, z + 1, c))


def send(a, pairs):
    return lax.ppermute(a, "gx", pairs)


def dot(a, b, ca, cb):
    return lax.dot_general(a, b, (((ca,), (cb,)), ((), ())), preferred_element_type=F32)


def place(pos, b):
    chip = ((b // 2 - pos[0]) & 3) * 2 + ((b & 1) ^ pos[1])
    row = ((PLACES >> (4 * chip)) & 7) * BLK
    return pl.ds(pl.multiple_of(row, BLK), BLK)


def whole(shape):
    return pl.BlockSpec(shape, lambda i, pos: (0,) * len(shape))


def params(mib):
    return pltpu.CompilerParams(vmem_limit_bytes=mib << 20, dimension_semantics=("arbitrary",))


def spread_kernel(tokens, out_grad, copies):
    for b in range(8):
        copies[b, :, :512] = tokens[...]
        copies[b, :, 512:] = out_grad[...]


def spread(tokens, out_grad):
    return pl.pallas_call(
        spread_kernel,
        out_shape=jax.ShapeDtypeStruct((8, BLK, 1024), BF),
        compiler_params=pltpu.CompilerParams(vmem_limit_bytes=58 << 20),
        cost_estimate=pl.CostEstimate(flops=0, bytes_accessed=1 << 20, transcendentals=0),
    )(tokens, out_grad)


def order_kernel(pos, blocks, tg, tok_t):
    for b in range(8):
        tg[place(pos, b), :] = blocks[b]
    tok_t[...] = tg[:, :512].T


def order(pos, blocks):
    return pl.pallas_call(
        order_kernel,
        grid_spec=pltpu.PrefetchScalarGridSpec(
            num_scalar_prefetch=1,
            grid=(1,),
            in_specs=[whole((8, BLK, 1024))],
            out_specs=[whole((512, 1024)), whole((512, 512))],
        ),
        out_shape=[jax.ShapeDtypeStruct((512, 1024), BF), jax.ShapeDtypeStruct((512, 512), BF)],
        compiler_params=params(40),
        cost_estimate=pl.CostEstimate(flops=0, bytes_accessed=4 << 20, transcendentals=0),
    )(pos, blocks)


def sums_kernel(part, pos, tg, tg_sib, gw, uw, dw, gw_sib, uw_sib, dw_sib, *outs):
    for a in range(3):
        if a < 2:
            own, sib = ((gw, gw_sib), (uw, uw_sib))[a]
            total = dot(tg[:, :512], own[...], 1, 0) + dot(tg_sib[:, :512], sib[...], 1, 0)
        else:
            total = dot(tg[:, 512:], dw[...], 1, 1) + dot(tg_sib[:, 512:], dw_sib[...], 1, 1)
        blocks = [total[i * BLK : (i + 1) * BLK] for i in range(4)]
        for block, out in zip(blocks[part == 0 :], outs):
            out[a] = block
        if part == 0:
            far, (z, up, down) = blocks[0].astype(BF), outs[3:]
            up_lo = MID - CUTS[0]

            @pl.when(pl.program_id(0) == 0)
            def _():
                z[a] = far[:, : CUTS[0]]
                up[a, :, :up_lo] = far[:, CUTS[0] :]

            @pl.when(pl.program_id(0) == 1)
            def _():
                up[a, :, up_lo:] = far[:, : CUTS[1] - MID]
                down[a] = far[:, CUTS[1] - MID :]


def sums(pos, tg, tg_sib, weights, weights_sib, part):
    tile = MID
    cols, rows = (512, tile), (tile, 512)
    own = lambda i, pos: (0, pos[2] * 2 + i)
    sib = lambda i, pos: (0, i)
    flip = lambda f: (lambda i, pos: f(i, pos)[::-1])
    tokens = pl.BlockSpec((256, 1024), lambda i, pos: (part, 0))
    kept = 3 if part == 0 else 4
    far = [(3, BLK, width) for width in TURN] if part == 0 else []
    return pl.pallas_call(
        functools.partial(sums_kernel, part),
        grid_spec=pltpu.PrefetchScalarGridSpec(
            num_scalar_prefetch=1,
            grid=(2,),
            in_specs=[
                tokens,
                tokens,
                pl.BlockSpec(cols, own),
                pl.BlockSpec(cols, own),
                pl.BlockSpec(rows, flip(own)),
                pl.BlockSpec(cols, sib),
                pl.BlockSpec(cols, sib),
                pl.BlockSpec(rows, flip(sib)),
            ],
            out_specs=[pl.BlockSpec((3, BLK, tile), lambda i, pos: (0, 0, i))] * kept
            + [whole(shape) for shape in far],
        ),
        out_shape=[jax.ShapeDtypeStruct((3, BLK, HALF), F32)] * kept
        + [jax.ShapeDtypeStruct(shape, BF) for shape in far],
        compiler_params=params(40),
        cost_estimate=pl.CostEstimate(
            flops=2 * 3 * 256 * 1024 * HALF, bytes_accessed=20 << 20, transcendentals=0
        ),
    )(pos, tg, tg_sib, *weights, *weights_sib)


PIECES = [pl.BlockSpec(memory_space=pl.ANY)] * 3
COPIES = 5


def stack(half, grads, near, mids, far, sems):
    arrays = pl.ds(0, grads.shape[0])
    columns = pl.ds(half * MID, MID)
    up, down, flat = 0, 1, 2
    ways = [(far, 0, 0, BLK), (near, 0, 4 * BLK, 4 * BLK)]
    for i, piece in enumerate((down, flat, up) if half else (up, down, flat)):
        ways.append((mids, piece * BLK, (i + 1) * BLK, BLK))
    copies = [
        pltpu.make_async_copy(
            source.at[arrays, pl.ds(at, size), columns], grads.at[:, pl.ds(to, size), :], sems.at[k]
        )
        for k, (source, at, to, size) in enumerate(ways)
    ]
    for copy in copies:
        copy.start()
    return copies


def wait(copies):
    for copy in copies:
        copy.wait()


def part_kernel(half, has_terms, has_weights, carried, last, pos, *refs):
    refs = list(refs)
    near, mids, far = (refs.pop(0) for _ in range(3))
    gw, uw = (refs.pop(0) for _ in range(2)) if has_terms else (None, None)
    before = refs.pop(0) if has_terms and carried else None
    tok_t, tg = (refs.pop(0) for _ in range(2)) if has_weights else (None, None)
    sems, grads = refs.pop(), refs.pop()
    acc = refs.pop() if has_terms else None
    wait(stack(half, grads, near, mids, far, sems))
    if has_weights:
        ggw, guw, gdw = refs[-3:]
        ggw[...] = dot(tok_t[...], grads[0], 1, 0).astype(BF)
        guw[...] = dot(tok_t[...], grads[1], 1, 0).astype(BF)
        gdw[...] = dot(grads[2], tg[:, 512:], 0, 0).astype(BF)
    if has_terms:
        out = refs[-4] if has_weights else refs[-1]
        term = dot(grads[0], gw[...], 1, 1) + dot(grads[1], uw[...], 1, 1)
        if carried:
            term += before[...]
        if not last:
            out[...] = term
        else:
            acc[...] = term
            for b in range(8):
                out[b] = acc[place(pos, b), :].astype(BF)


def part(pos, pieces, core, half, terms=None, weights=None, last=False):
    tile = lambda pos: (core ^ pos[2]) * 2 + half
    arrays = 3 if weights else 2
    column = pl.BlockSpec((512, MID), lambda i, pos: (0, tile(pos)))
    row = pl.BlockSpec((MID, 512), lambda i, pos: (tile(pos), 0))
    square = whole((512, 512))
    in_specs = [*PIECES]
    args, out_specs, out_shape, scratch, aliases = [*pieces], [], [], [], {}
    carried = False
    if terms:
        gw, uw, before = terms
        in_specs += [column, column]
        args += [gw, uw]
        carried = before is not None
        if carried:
            in_specs.append(square)
            args.append(before)
        if last:
            out_specs.append(whole((8, BLK, 512)))
            out_shape.append(jax.ShapeDtypeStruct((8, BLK, 512), BF))
        else:
            out_specs.append(square)
            out_shape.append(jax.ShapeDtypeStruct((512, 512), F32))
        scratch.append(pltpu.VMEM((512, 512), F32))
    if weights:
        tok_t, tg, beside = weights
        in_specs += [square, whole((512, 1024))]
        args += [tok_t, tg]
        if beside is not None:
            for k in range(3):
                aliases[len(args) + 1 + k] = len(out_specs) + k
            in_specs += [pl.BlockSpec(memory_space=pl.ANY)] * 3
            args += beside
        out_specs += [column, column, row]
        out_shape += [jax.ShapeDtypeStruct((512, 2 * HALF), BF)] * 2
        out_shape += [jax.ShapeDtypeStruct((2 * HALF, 512), BF)]
    scratch += [pltpu.VMEM((arrays, 512, MID), BF), pltpu.SemaphoreType.DMA((COPIES,))]
    flops = 2 * 512 * 512 * MID * (2 * bool(terms) + 3 * bool(weights))
    return pl.pallas_call(
        functools.partial(part_kernel, half, bool(terms), bool(weights), carried, last),
        grid_spec=pltpu.PrefetchScalarGridSpec(
            num_scalar_prefetch=1,
            grid=(1,),
            in_specs=in_specs,
            out_specs=out_specs,
            scratch_shapes=scratch,
        ),
        out_shape=out_shape,
        input_output_aliases=aliases,
        compiler_params=params(32),
        cost_estimate=pl.CostEstimate(flops=flops, bytes_accessed=8 << 20, transcendentals=0),
    )(pos, *args)


def total_kernel(terms, out):
    total = wide(terms[0])
    for b in range(1, 8):
        total += wide(terms[b])
    out[...] = total.astype(BF)


def total_of(terms):
    return pl.pallas_call(
        total_kernel,
        out_shape=jax.ShapeDtypeStruct((BLK, 512), BF),
        compiler_params=pltpu.CompilerParams(vmem_limit_bytes=8 << 20),
        cost_estimate=pl.CostEstimate(flops=1 << 18, bytes_accessed=1 << 19, transcendentals=0),
    )(terms)


def wide(a):
    return a.astype(F32)


def lo(a):
    return a[..., :MID]


def hi(a):
    return a[..., MID:]


def join(*parts):
    return jnp.concatenate(parts, axis=-1)


def merge_kernel(p20, p11, p31, rz, rp, rm, down, up, flat):
    z, x = CUTS
    for a in range(3):
        down[a, :, :z] = (p20[a, :, :z] + wide(rz[a])).astype(BF)
        down[a, :, z:MID] = p20[a, :, z:MID].astype(BF)
        down[a, :, MID:x] = p31[a, :, MID:x].astype(BF)
        down[a, :, x:] = (p31[a, :, x:] + wide(rm[a])).astype(BF)
        up[a, :, :z] = p11[a, :, :z].astype(BF)
        up[a, :, z:MID] = (p11[a, :, z:MID] + wide(rp[a, :, : MID - z])).astype(BF)
        up[a, :, MID:] = p20[a, :, MID:].astype(BF)
        flat[a, :, :MID] = p31[a, :, :MID].astype(BF)
        flat[a, :, MID:x] = (p11[a, :, MID:x] + wide(rp[a, :, MID - z :])).astype(BF)
        flat[a, :, x:] = p11[a, :, x:].astype(BF)


def scatter_far(p20, p11, p31, far_z, far_up, far_down):
    return pl.pallas_call(
        merge_kernel,
        out_shape=[jax.ShapeDtypeStruct((3, BLK, HALF), BF)] * 3,
        compiler_params=pltpu.CompilerParams(vmem_limit_bytes=32 << 20),
        cost_estimate=pl.CostEstimate(flops=0, bytes_accessed=6 << 20, transcendentals=0),
    )(p20, p11, p31, send(far_z, ZS), send(far_up, XP), send(far_down, XM))


def scatter_mid(down, up, flat, p10, p30, p01):
    rm, rp, rz = wide(send(down, XM)), wide(send(up, XP)), wide(send(flat, ZS))
    p10 = join(lo(p10), hi(p10) + hi(rp) + hi(rz))
    p30 = join(lo(p30) + lo(rm) + lo(rz), hi(p30))
    p01 = join(lo(p01) + lo(rp), hi(p01) + hi(rm))
    return p10.astype(BF), p30.astype(BF), p01.astype(BF)


def scatter_last(up, down, flat, p00):
    rp, rm, rz = send(up, XP), send(down, XM), send(flat, ZS)
    return p00 + wide(rp) + wide(rm) + wide(rz)


def rows(*blocks):
    return jnp.concatenate(blocks, axis=-2)


def after(*arrays):
    return lax.optimization_barrier(arrays)


def gather(e):
    z, x = CUTS
    g30, g10, g01 = send(e, XP), send(e, XM), send(e, ZS)
    rp = send(join(lo(g30), hi(g01)), XP)
    rm = send(join(lo(g01), hi(g10)), XM)
    rz = send(join(lo(g30), hi(g10)), ZS)
    rm, near = after(rm, rows(g10, g30, g01, e))
    turn_up = join(rz[..., z:MID], rp[..., MID:x])
    fz, fp, fm = send(rp[..., :z], ZS), send(turn_up, XP), send(rz[..., x:], XM)
    far, mids = after(join(fz, fp, fm), rows(rp, rm, rz))
    pieces = near, mids, far
    return pieces, [send(piece, CORE) for piece in pieces]


def local_grads(gate_sum, upper_sum, back_sum):
    sigmoid_gate = jax.nn.sigmoid(gate_sum)
    silu_gate = gate_sum * sigmoid_gate
    hidden = (silu_gate * upper_sum).astype(BF)
    grad_gate = (
        back_sum * upper_sum * sigmoid_gate * (1.0 + gate_sum * (1.0 - sigmoid_gate))
    ).astype(BF)
    grad_upper = (back_sum * silu_gate).astype(BF)
    return jnp.stack([grad_gate, grad_upper, hidden])


def shards(tokens, out_grad, gate_weight, up_weight, down_weight):
    gx = lax.axis_index("gx")
    core = gx % 2
    pos = jnp.stack([gx // 4, (gx // 2) % 2, core]).astype(jnp.int32)
    far_half = (1 - core) * HALF

    blocks = lax.all_to_all(spread(tokens, out_grad), "gy", 0, 0, tiled=True)
    weights = (gate_weight, up_weight, down_weight)
    weights_sib = [
        send(lax.dynamic_slice_in_dim(w, far_half, HALF, axis), CORE)
        for w, axis in zip(weights, (1, 1, 0))
    ]
    tg, tok_t = order(pos, blocks)
    tg_sib = send(tg, CORE)

    first = sums(pos, tg, tg_sib, weights, weights_sib, 0)
    p10, p30, p01, p00 = sums(pos, tg, tg_sib, weights, weights_sib, 1)
    mid = scatter_far(*first)
    last = scatter_mid(*mid, p10, p30, p01)
    total = scatter_last(*last, p00)
    own, sib = gather(local_grads(total[0], total[1], total[2]))

    gw, uw = gate_weight, up_weight
    terms, *grads = part(pos, own, 0, 0, (gw, uw, None), (tok_t, tg, None))
    terms, *grads = part(pos, own, 0, 1, (gw, uw, terms), (tok_t, tg, grads))
    (terms,) = part(pos, sib, 1, 0, (gw, uw, terms))
    (terms,) = part(pos, sib, 1, 1, (gw, uw, terms), None, True)
    grad_tokens = total_of(lax.all_to_all(terms, "gy", 0, 0, tiled=True))
    grads = part(pos, sib, 1, 0, None, (tok_t, tg, grads))
    ggw, guw, gdw = part(pos, sib, 1, 1, None, (tok_t, tg, grads))
    return grad_tokens, ggw, guw, gdw


def solution(mesh):
    return jax.shard_map(
        shards,
        mesh=mesh,
        in_specs=(P("gy", "gx"), P("gy", "gx"), P("gx", "gy"), P("gx", "gy"), P("gy", "gx")),
        out_specs=(P("gy", "gx"), P("gx", "gy"), P("gx", "gy"), P("gy", "gx")),
        check_vma=False,
    )
```

```python
import functools

import jax
import jax.numpy as jnp
from jax import lax
from jax.experimental import pallas as pl
from jax.experimental.pallas import tpu as pltpu
from jax.sharding import PartitionSpec as P

BF, F32 = jnp.bfloat16, jnp.float32
BLK = 64
TILE = 256
HALF = 7 * TILE
CUTS = (512, 1152)
MID = HALF // 2
TURN = CUTS[0], CUTS[1] - CUTS[0], HALF - CUTS[1]
ORDER = ((2, 1), (2, 0), (1, 1), (3, 1), (1, 0), (3, 0), (0, 1), (0, 0))
PLACES = sum(i << 4 * (2 * jx + jz) for i, (jx, jz) in enumerate(ORDER))


def gx_perm(move):
    pairs = []
    for i in range(16):
        x, z, c = move(i // 4, (i // 2) % 2, i % 2)
        pairs.append((i, (x % 4) * 4 + (z % 2) * 2 + c % 2))
    return pairs


CORE = gx_perm(lambda x, z, c: (x, z, c + 1))
XP = gx_perm(lambda x, z, c: (x + 1, z, c))
XM = gx_perm(lambda x, z, c: (x - 1, z, c))
ZS = gx_perm(lambda x, z, c: (x, z + 1, c))


def send(a, pairs):
    return lax.ppermute(a, "gx", pairs)


def dot(a, b, ca, cb):
    return lax.dot_general(a, b, (((ca,), (cb,)), ((), ())), preferred_element_type=F32)


def place(pos, b):
    chip = ((b // 2 - pos[0]) & 3) * 2 + ((b & 1) ^ pos[1])
    row = ((PLACES >> (4 * chip)) & 7) * BLK
    return pl.ds(pl.multiple_of(row, BLK), BLK)


def whole(shape):
    return pl.BlockSpec(shape, lambda i, pos: (0,) * len(shape))


def params(mib):
    return pltpu.CompilerParams(vmem_limit_bytes=mib << 20, dimension_semantics=("arbitrary",))


def spread_kernel(tokens, out_grad, copies):
    for b in range(8):
        copies[b, :, :512] = tokens[...]
        copies[b, :, 512:] = out_grad[...]


def spread(tokens, out_grad):
    return pl.pallas_call(
        spread_kernel,
        out_shape=jax.ShapeDtypeStruct((8, BLK, 1024), BF),
        compiler_params=pltpu.CompilerParams(vmem_limit_bytes=58 << 20),
        cost_estimate=pl.CostEstimate(flops=0, bytes_accessed=1 << 20, transcendentals=0),
    )(tokens, out_grad)


def order_kernel(pos, blocks, tg, tok_t):
    for b in range(8):
        tg[place(pos, b), :] = blocks[b]
    tok_t[...] = tg[:, :512].T


def order(pos, blocks):
    return pl.pallas_call(
        order_kernel,
        grid_spec=pltpu.PrefetchScalarGridSpec(
            num_scalar_prefetch=1,
            grid=(1,),
            in_specs=[whole((8, BLK, 1024))],
            out_specs=[whole((512, 1024)), whole((512, 512))],
        ),
        out_shape=[jax.ShapeDtypeStruct((512, 1024), BF), jax.ShapeDtypeStruct((512, 512), BF)],
        compiler_params=params(40),
        cost_estimate=pl.CostEstimate(flops=0, bytes_accessed=4 << 20, transcendentals=0),
    )(pos, blocks)


def sums_kernel(part, pos, tg, tg_sib, gw, uw, dw, gw_sib, uw_sib, dw_sib, *outs):
    for a in range(3):
        if a < 2:
            own, sib = ((gw, gw_sib), (uw, uw_sib))[a]
            total = dot(tg[:, :512], own[...], 1, 0) + dot(tg_sib[:, :512], sib[...], 1, 0)
        else:
            total = dot(tg[:, 512:], dw[...], 1, 1) + dot(tg_sib[:, 512:], dw_sib[...], 1, 1)
        blocks = [total[i * BLK : (i + 1) * BLK] for i in range(4)]
        for block, out in zip(blocks[part == 0 :], outs):
            out[a] = block
        if part == 0:
            far, (z, up, down) = blocks[0].astype(BF), outs[3:]
            up_lo = MID - CUTS[0]

            @pl.when(pl.program_id(0) == 0)
            def _():
                z[a] = far[:, : CUTS[0]]
                up[a, :, :up_lo] = far[:, CUTS[0] :]

            @pl.when(pl.program_id(0) == 1)
            def _():
                up[a, :, up_lo:] = far[:, : CUTS[1] - MID]
                down[a] = far[:, CUTS[1] - MID :]


def sums(pos, tg, tg_sib, weights, weights_sib, part):
    tile = MID
    cols, rows = (512, tile), (tile, 512)
    own = lambda i, pos: (0, pos[2] * 2 + i)
    sib = lambda i, pos: (0, i)
    flip = lambda f: (lambda i, pos: f(i, pos)[::-1])
    tokens = pl.BlockSpec((256, 1024), lambda i, pos: (part, 0))
    kept = 3 if part == 0 else 4
    far = [(3, BLK, width) for width in TURN] if part == 0 else []
    return pl.pallas_call(
        functools.partial(sums_kernel, part),
        grid_spec=pltpu.PrefetchScalarGridSpec(
            num_scalar_prefetch=1,
            grid=(2,),
            in_specs=[
                tokens,
                tokens,
                pl.BlockSpec(cols, own),
                pl.BlockSpec(cols, own),
                pl.BlockSpec(rows, flip(own)),
                pl.BlockSpec(cols, sib),
                pl.BlockSpec(cols, sib),
                pl.BlockSpec(rows, flip(sib)),
            ],
            out_specs=[pl.BlockSpec((3, BLK, tile), lambda i, pos: (0, 0, i))] * kept
            + [whole(shape) for shape in far],
        ),
        out_shape=[jax.ShapeDtypeStruct((3, BLK, HALF), F32)] * kept
        + [jax.ShapeDtypeStruct(shape, BF) for shape in far],
        compiler_params=params(40),
        cost_estimate=pl.CostEstimate(
            flops=2 * 3 * 256 * 1024 * HALF, bytes_accessed=20 << 20, transcendentals=0
        ),
    )(pos, tg, tg_sib, *weights, *weights_sib)


PIECES = [pl.BlockSpec(memory_space=pl.ANY)] * 3
COPIES = 5


def stack(half, grads, near, mids, far, sems):
    arrays = pl.ds(0, grads.shape[0])
    columns = pl.ds(half * MID, MID)
    up, down, flat = 0, 1, 2
    ways = [(far, 0, 0, BLK), (near, 0, 4 * BLK, 4 * BLK)]
    for i, piece in enumerate((down, flat, up) if half else (up, down, flat)):
        ways.append((mids, piece * BLK, (i + 1) * BLK, BLK))
    copies = [
        pltpu.make_async_copy(
            source.at[arrays, pl.ds(at, size), columns], grads.at[:, pl.ds(to, size), :], sems.at[k]
        )
        for k, (source, at, to, size) in enumerate(ways)
    ]
    for copy in copies:
        copy.start()
    return copies


def wait(copies):
    for copy in copies:
        copy.wait()


def part_kernel(half, has_terms, has_weights, carried, last, pos, *refs):
    refs = list(refs)
    near, mids, far = (refs.pop(0) for _ in range(3))
    gw, uw = (refs.pop(0) for _ in range(2)) if has_terms else (None, None)
    before = refs.pop(0) if has_terms and carried else None
    tok_t, tg = (refs.pop(0) for _ in range(2)) if has_weights else (None, None)
    sems, grads = refs.pop(), refs.pop()
    acc = refs.pop() if has_terms else None
    wait(stack(half, grads, near, mids, far, sems))
    if has_weights:
        ggw, guw, gdw = refs[-3:]
        ggw[...] = dot(tok_t[...], grads[0], 1, 0).astype(BF)
        guw[...] = dot(tok_t[...], grads[1], 1, 0).astype(BF)
        gdw[...] = dot(grads[2], tg[:, 512:], 0, 0).astype(BF)
    if has_terms:
        out = refs[-4] if has_weights else refs[-1]
        term = dot(grads[0], gw[...], 1, 1) + dot(grads[1], uw[...], 1, 1)
        if carried:
            term += before[...]
        if not last:
            out[...] = term
        else:
            acc[...] = term
            for b in range(8):
                out[b] = acc[place(pos, b), :]


def part(pos, pieces, core, half, terms=None, weights=None, last=False):
    tile = lambda pos: (core ^ pos[2]) * 2 + half
    arrays = 3 if weights else 2
    column = pl.BlockSpec((512, MID), lambda i, pos: (0, tile(pos)))
    row = pl.BlockSpec((MID, 512), lambda i, pos: (tile(pos), 0))
    square = whole((512, 512))
    in_specs = [*PIECES]
    args, out_specs, out_shape, scratch, aliases = [*pieces], [], [], [], {}
    carried = False
    if terms:
        gw, uw, before = terms
        in_specs += [column, column]
        args += [gw, uw]
        carried = before is not None
        if carried:
            in_specs.append(square)
            args.append(before)
        if last:
            out_specs.append(whole((8, BLK, 512)))
            out_shape.append(jax.ShapeDtypeStruct((8, BLK, 512), F32))
        else:
            out_specs.append(square)
            out_shape.append(jax.ShapeDtypeStruct((512, 512), F32))
        scratch.append(pltpu.VMEM((512, 512), F32))
    if weights:
        tok_t, tg, beside = weights
        in_specs += [square, whole((512, 1024))]
        args += [tok_t, tg]
        if beside is not None:
            for k in range(3):
                aliases[len(args) + 1 + k] = len(out_specs) + k
            in_specs += [pl.BlockSpec(memory_space=pl.ANY)] * 3
            args += beside
        out_specs += [column, column, row]
        out_shape += [jax.ShapeDtypeStruct((512, 2 * HALF), BF)] * 2
        out_shape += [jax.ShapeDtypeStruct((2 * HALF, 512), BF)]
    scratch += [pltpu.VMEM((arrays, 512, MID), BF), pltpu.SemaphoreType.DMA((COPIES,))]
    flops = 2 * 512 * 512 * MID * (2 * bool(terms) + 3 * bool(weights))
    return pl.pallas_call(
        functools.partial(part_kernel, half, bool(terms), bool(weights), carried, last),
        grid_spec=pltpu.PrefetchScalarGridSpec(
            num_scalar_prefetch=1,
            grid=(1,),
            in_specs=in_specs,
            out_specs=out_specs,
            scratch_shapes=scratch,
        ),
        out_shape=out_shape,
        input_output_aliases=aliases,
        compiler_params=params(32),
        cost_estimate=pl.CostEstimate(flops=flops, bytes_accessed=8 << 20, transcendentals=0),
    )(pos, *args)


def total_kernel(terms, out):
    total = wide(terms[0])
    for b in range(1, 8):
        total += wide(terms[b])
    out[...] = total.astype(BF)


def total_of(terms):
    return pl.pallas_call(
        total_kernel,
        out_shape=jax.ShapeDtypeStruct((BLK, 512), BF),
        compiler_params=pltpu.CompilerParams(vmem_limit_bytes=8 << 20),
        cost_estimate=pl.CostEstimate(flops=1 << 18, bytes_accessed=1 << 19, transcendentals=0),
    )(terms)


def wide(a):
    return a.astype(F32)


def lo(a):
    return a[..., :MID]


def hi(a):
    return a[..., MID:]


def join(*parts):
    return jnp.concatenate(parts, axis=-1)


def merge_kernel(p20, p11, p31, rz, rp, rm, down, up, flat):
    z, x = CUTS
    for a in range(3):
        down[a, :, :z] = (p20[a, :, :z] + wide(rz[a])).astype(BF)
        down[a, :, z:MID] = p20[a, :, z:MID].astype(BF)
        down[a, :, MID:x] = p31[a, :, MID:x].astype(BF)
        down[a, :, x:] = (p31[a, :, x:] + wide(rm[a])).astype(BF)
        up[a, :, :z] = p11[a, :, :z].astype(BF)
        up[a, :, z:MID] = (p11[a, :, z:MID] + wide(rp[a, :, : MID - z])).astype(BF)
        up[a, :, MID:] = p20[a, :, MID:].astype(BF)
        flat[a, :, :MID] = p31[a, :, :MID].astype(BF)
        flat[a, :, MID:x] = (p11[a, :, MID:x] + wide(rp[a, :, MID - z :])).astype(BF)
        flat[a, :, x:] = p11[a, :, x:].astype(BF)


def scatter_far(p20, p11, p31, far_z, far_up, far_down):
    return pl.pallas_call(
        merge_kernel,
        out_shape=[jax.ShapeDtypeStruct((3, BLK, HALF), BF)] * 3,
        compiler_params=pltpu.CompilerParams(vmem_limit_bytes=32 << 20),
        cost_estimate=pl.CostEstimate(flops=0, bytes_accessed=6 << 20, transcendentals=0),
    )(p20, p11, p31, send(far_z, ZS), send(far_up, XP), send(far_down, XM))


def scatter_mid(down, up, flat, p10, p30, p01):
    rm, rp, rz = wide(send(down, XM)), wide(send(up, XP)), wide(send(flat, ZS))
    p10 = join(lo(p10), hi(p10) + hi(rp) + hi(rz))
    p30 = join(lo(p30) + lo(rm) + lo(rz), hi(p30))
    p01 = join(lo(p01) + lo(rp), hi(p01) + hi(rm))
    return p10.astype(BF), p30.astype(BF), p01.astype(BF)


def scatter_last(up, down, flat, p00):
    rp, rm, rz = send(up, XP), send(down, XM), send(flat, ZS)
    return p00 + wide(rp) + wide(rm) + wide(rz)


def rows(*blocks):
    return jnp.concatenate(blocks, axis=-2)


def after(*arrays):
    return lax.optimization_barrier(arrays)


def gather(e):
    z, x = CUTS
    g30, g10, g01 = send(e, XP), send(e, XM), send(e, ZS)
    rp = send(join(lo(g30), hi(g01)), XP)
    rm = send(join(lo(g01), hi(g10)), XM)
    rz = send(join(lo(g30), hi(g10)), ZS)
    rm, near = after(rm, rows(g10, g30, g01, e))
    turn_up = join(rz[..., z:MID], rp[..., MID:x])
    fz, fp, fm = send(rp[..., :z], ZS), send(turn_up, XP), send(rz[..., x:], XM)
    far, mids = after(join(fz, fp, fm), rows(rp, rm, rz))
    pieces = near, mids, far
    return pieces, [send(piece, CORE) for piece in pieces]


def local_grads(gate_sum, upper_sum, back_sum):
    sigmoid_gate = jax.nn.sigmoid(gate_sum)
    silu_gate = gate_sum * sigmoid_gate
    hidden = (silu_gate * upper_sum).astype(BF)
    grad_gate = (
        back_sum * upper_sum * sigmoid_gate * (1.0 + gate_sum * (1.0 - sigmoid_gate))
    ).astype(BF)
    grad_upper = (back_sum * silu_gate).astype(BF)
    return jnp.stack([grad_gate, grad_upper, hidden])


def shards(tokens, out_grad, gate_weight, up_weight, down_weight):
    gx = lax.axis_index("gx")
    core = gx % 2
    pos = jnp.stack([gx // 4, (gx // 2) % 2, core]).astype(jnp.int32)
    far_half = (1 - core) * HALF

    blocks = lax.all_to_all(spread(tokens, out_grad), "gy", 0, 0, tiled=True)
    weights = (gate_weight, up_weight, down_weight)
    weights_sib = [
        send(lax.dynamic_slice_in_dim(w, far_half, HALF, axis), CORE)
        for w, axis in zip(weights, (1, 1, 0))
    ]
    tg, tok_t = order(pos, blocks)
    tg_sib = send(tg, CORE)

    first = sums(pos, tg, tg_sib, weights, weights_sib, 0)
    p10, p30, p01, p00 = sums(pos, tg, tg_sib, weights, weights_sib, 1)
    mid = scatter_far(*first)
    last = scatter_mid(*mid, p10, p30, p01)
    total = scatter_last(*last, p00)
    own, sib = gather(local_grads(total[0], total[1], total[2]))

    gw, uw = gate_weight, up_weight
    terms, *grads = part(pos, own, 0, 0, (gw, uw, None), (tok_t, tg, None))
    terms, *grads = part(pos, own, 0, 1, (gw, uw, terms), (tok_t, tg, grads))
    (terms,) = part(pos, sib, 1, 0, (gw, uw, terms))
    (terms,) = part(pos, sib, 1, 1, (gw, uw, terms), None, True)
    grad_tokens = total_of(lax.all_to_all(terms, "gy", 0, 0, tiled=True))
    grads = part(pos, sib, 1, 0, None, (tok_t, tg, grads))
    ggw, guw, gdw = part(pos, sib, 1, 1, None, (tok_t, tg, grads))
    return grad_tokens, ggw, guw, gdw


def solution(mesh):
    return jax.shard_map(
        shards,
        mesh=mesh,
        in_specs=(P("gy", "gx"), P("gy", "gx"), P("gx", "gy"), P("gx", "gy"), P("gy", "gx")),
        out_specs=(P("gy", "gx"), P("gx", "gy"), P("gx", "gy"), P("gy", "gx")),
        check_vma=False,
    )
```

```python
import functools

import jax
import jax.numpy as jnp
from jax import lax
from jax.experimental import pallas as pl
from jax.experimental.pallas import tpu as pltpu
from jax.sharding import PartitionSpec as P

BF, F32 = jnp.bfloat16, jnp.float32
BLK = 64
TILE = 256
HALF = 7 * TILE
CUTS = (512, 1152)
MID = HALF // 2
TURN = CUTS[0], CUTS[1] - CUTS[0], HALF - CUTS[1]
ORDER = ((2, 1), (2, 0), (1, 1), (3, 1), (1, 0), (3, 0), (0, 1), (0, 0))
PLACES = sum(i << 4 * (2 * jx + jz) for i, (jx, jz) in enumerate(ORDER))


def gx_perm(move):
    pairs = []
    for i in range(16):
        x, z, c = move(i // 4, (i // 2) % 2, i % 2)
        pairs.append((i, (x % 4) * 4 + (z % 2) * 2 + c % 2))
    return pairs


CORE = gx_perm(lambda x, z, c: (x, z, c + 1))
XP = gx_perm(lambda x, z, c: (x + 1, z, c))
XM = gx_perm(lambda x, z, c: (x - 1, z, c))
ZS = gx_perm(lambda x, z, c: (x, z + 1, c))


def send(a, pairs):
    return lax.ppermute(a, "gx", pairs)


def dot(a, b, ca, cb):
    return lax.dot_general(a, b, (((ca,), (cb,)), ((), ())), preferred_element_type=F32)


def place(pos, b):
    chip = ((b // 2 - pos[0]) & 3) * 2 + ((b & 1) ^ pos[1])
    row = ((PLACES >> (4 * chip)) & 7) * BLK
    return pl.ds(pl.multiple_of(row, BLK), BLK)


def whole(shape):
    return pl.BlockSpec(shape, lambda i, pos: (0,) * len(shape))


def params(mib):
    return pltpu.CompilerParams(vmem_limit_bytes=mib << 20, dimension_semantics=("arbitrary",))


def spread_kernel(tokens, out_grad, copies):
    for b in range(8):
        copies[b, :, :512] = tokens[...]
        copies[b, :, 512:] = out_grad[...]


def spread(tokens, out_grad):
    return pl.pallas_call(
        spread_kernel,
        out_shape=jax.ShapeDtypeStruct((8, BLK, 1024), BF),
        compiler_params=pltpu.CompilerParams(vmem_limit_bytes=58 << 20),
        cost_estimate=pl.CostEstimate(flops=0, bytes_accessed=1 << 20, transcendentals=0),
    )(tokens, out_grad)


def order_kernel(pos, blocks, tg, tok_t):
    for b in range(8):
        tg[place(pos, b), :] = blocks[b]
    tok_t[...] = tg[:, :512].T


def order(pos, blocks):
    return pl.pallas_call(
        order_kernel,
        grid_spec=pltpu.PrefetchScalarGridSpec(
            num_scalar_prefetch=1,
            grid=(1,),
            in_specs=[whole((8, BLK, 1024))],
            out_specs=[whole((512, 1024)), whole((512, 512))],
        ),
        out_shape=[jax.ShapeDtypeStruct((512, 1024), BF), jax.ShapeDtypeStruct((512, 512), BF)],
        compiler_params=params(40),
        cost_estimate=pl.CostEstimate(flops=0, bytes_accessed=4 << 20, transcendentals=0),
    )(pos, blocks)


def sums_kernel(part, pos, tg, tg_sib, gw, uw, dw, gw_sib, uw_sib, dw_sib, *outs):
    for a in range(3):
        if a < 2:
            own, sib = ((gw, gw_sib), (uw, uw_sib))[a]
            total = dot(tg[:, :512], own[...], 1, 0) + dot(tg_sib[:, :512], sib[...], 1, 0)
        else:
            total = dot(tg[:, 512:], dw[...], 1, 1) + dot(tg_sib[:, 512:], dw_sib[...], 1, 1)
        blocks = [total[i * BLK : (i + 1) * BLK] for i in range(4)]
        for block, out in zip(blocks[part == 0 :], outs):
            out[a] = block
        if part == 0:
            far, (z, up, down) = blocks[0].astype(BF), outs[3:]
            up_lo = MID - CUTS[0]

            @pl.when(pl.program_id(0) == 0)
            def _():
                z[a] = far[:, : CUTS[0]]
                up[a, :, :up_lo] = far[:, CUTS[0] :]

            @pl.when(pl.program_id(0) == 1)
            def _():
                up[a, :, up_lo:] = far[:, : CUTS[1] - MID]
                down[a] = far[:, CUTS[1] - MID :]


def sums(pos, tg, tg_sib, weights, weights_sib, part):
    tile = MID
    cols, rows = (512, tile), (tile, 512)
    own = lambda i, pos: (0, pos[2] * 2 + i)
    sib = lambda i, pos: (0, i)
    flip = lambda f: (lambda i, pos: f(i, pos)[::-1])
    tokens = pl.BlockSpec((256, 1024), lambda i, pos: (part, 0))
    kept = 3 if part == 0 else 4
    far = [(3, BLK, width) for width in TURN] if part == 0 else []
    return pl.pallas_call(
        functools.partial(sums_kernel, part),
        grid_spec=pltpu.PrefetchScalarGridSpec(
            num_scalar_prefetch=1,
            grid=(2,),
            in_specs=[
                tokens,
                tokens,
                pl.BlockSpec(cols, own),
                pl.BlockSpec(cols, own),
                pl.BlockSpec(rows, flip(own)),
                pl.BlockSpec(cols, sib),
                pl.BlockSpec(cols, sib),
                pl.BlockSpec(rows, flip(sib)),
            ],
            out_specs=[pl.BlockSpec((3, BLK, tile), lambda i, pos: (0, 0, i))] * kept
            + [whole(shape) for shape in far],
        ),
        out_shape=[jax.ShapeDtypeStruct((3, BLK, HALF), F32)] * kept
        + [jax.ShapeDtypeStruct(shape, BF) for shape in far],
        compiler_params=params(40),
        cost_estimate=pl.CostEstimate(
            flops=2 * 3 * 256 * 1024 * HALF, bytes_accessed=20 << 20, transcendentals=0
        ),
    )(pos, tg, tg_sib, *weights, *weights_sib)


PIECES = [pl.BlockSpec(memory_space=pl.ANY)] * 3
COPIES = 5


def stack(half, grads, near, mids, far, sems):
    arrays = pl.ds(0, grads.shape[0])
    columns = pl.ds(half * MID, MID)
    up, down, flat = 0, 1, 2
    ways = [(far, 0, 0, BLK), (near, 0, 4 * BLK, 4 * BLK)]
    for i, piece in enumerate((down, flat, up) if half else (up, down, flat)):
        ways.append((mids, piece * BLK, (i + 1) * BLK, BLK))
    copies = [
        pltpu.make_async_copy(
            source.at[arrays, pl.ds(at, size), columns], grads.at[:, pl.ds(to, size), :], sems.at[k]
        )
        for k, (source, at, to, size) in enumerate(ways)
    ]
    for copy in copies:
        copy.start()
    return copies


def wait(copies):
    for copy in copies:
        copy.wait()


def part_kernel(half, has_terms, has_weights, carried, last, pos, *refs):
    refs = list(refs)
    near, mids, far = (refs.pop(0) for _ in range(3))
    gw, uw = (refs.pop(0) for _ in range(2)) if has_terms else (None, None)
    before = refs.pop(0) if has_terms and carried else None
    tok_t, tg = (refs.pop(0) for _ in range(2)) if has_weights else (None, None)
    sems, grads = refs.pop(), refs.pop()
    acc = refs.pop() if has_terms else None
    wait(stack(half, grads, near, mids, far, sems))
    if has_weights:
        ggw, guw, gdw = refs[-3:]
        ggw[...] = dot(tok_t[...], grads[0], 1, 0).astype(BF)
        guw[...] = dot(tok_t[...], grads[1], 1, 0).astype(BF)
        gdw[...] = dot(grads[2], tg[...], 0, 0).astype(BF)
    if has_terms:
        out = refs[-4] if has_weights else refs[-1]
        term = dot(grads[0], gw[...], 1, 1) + dot(grads[1], uw[...], 1, 1)
        if carried:
            term += before[...]
        if not last:
            out[...] = term
        else:
            acc[...] = term
            for b in range(8):
                out[b] = acc[place(pos, b), :].astype(BF)


def part(pos, pieces, core, half, terms=None, weights=None, last=False):
    tile = lambda pos: (core ^ pos[2]) * 2 + half
    arrays = 3 if weights else 2
    column = pl.BlockSpec((512, MID), lambda i, pos: (0, tile(pos)))
    row = pl.BlockSpec((MID, 512), lambda i, pos: (tile(pos), 0))
    square = whole((512, 512))
    in_specs = [*PIECES]
    args, out_specs, out_shape, scratch, aliases = [*pieces], [], [], [], {}
    carried = False
    if terms:
        gw, uw, before = terms
        in_specs += [column, column]
        args += [gw, uw]
        carried = before is not None
        if carried:
            in_specs.append(square)
            args.append(before)
        if last:
            out_specs.append(whole((8, BLK, 512)))
            out_shape.append(jax.ShapeDtypeStruct((8, BLK, 512), BF))
        else:
            out_specs.append(square)
            out_shape.append(jax.ShapeDtypeStruct((512, 512), F32))
        scratch.append(pltpu.VMEM((512, 512), F32))
    if weights:
        tok_t, tg, beside = weights
        in_specs += [square, pl.BlockSpec((512, 512), lambda i, pos: (0, 1))]
        args += [tok_t, tg]
        if beside is not None:
            for k in range(3):
                aliases[len(args) + 1 + k] = len(out_specs) + k
            in_specs += [pl.BlockSpec(memory_space=pl.ANY)] * 3
            args += beside
        out_specs += [column, column, row]
        out_shape += [jax.ShapeDtypeStruct((512, 2 * HALF), BF)] * 2
        out_shape += [jax.ShapeDtypeStruct((2 * HALF, 512), BF)]
    scratch += [pltpu.VMEM((arrays, 512, MID), BF), pltpu.SemaphoreType.DMA((COPIES,))]
    flops = 2 * 512 * 512 * MID * (2 * bool(terms) + 3 * bool(weights))
    return pl.pallas_call(
        functools.partial(part_kernel, half, bool(terms), bool(weights), carried, last),
        grid_spec=pltpu.PrefetchScalarGridSpec(
            num_scalar_prefetch=1,
            grid=(1,),
            in_specs=in_specs,
            out_specs=out_specs,
            scratch_shapes=scratch,
        ),
        out_shape=out_shape,
        input_output_aliases=aliases,
        compiler_params=params(32),
        cost_estimate=pl.CostEstimate(flops=flops, bytes_accessed=8 << 20, transcendentals=0),
    )(pos, *args)


def total_kernel(terms, out):
    total = wide(terms[0])
    for b in range(1, 8):
        total += wide(terms[b])
    out[...] = total.astype(BF)


def total_of(terms):
    return pl.pallas_call(
        total_kernel,
        out_shape=jax.ShapeDtypeStruct((BLK, 512), BF),
        compiler_params=pltpu.CompilerParams(vmem_limit_bytes=8 << 20),
        cost_estimate=pl.CostEstimate(flops=1 << 18, bytes_accessed=1 << 19, transcendentals=0),
    )(terms)


def wide(a):
    return a.astype(F32)


def lo(a):
    return a[..., :MID]


def hi(a):
    return a[..., MID:]


def join(*parts):
    return jnp.concatenate(parts, axis=-1)


def merge_kernel(p20, p11, p31, rz, rp, rm, down, up, flat):
    z, x = CUTS
    for a in range(3):
        down[a, :, :z] = (p20[a, :, :z] + wide(rz[a])).astype(BF)
        down[a, :, z:MID] = p20[a, :, z:MID].astype(BF)
        down[a, :, MID:x] = p31[a, :, MID:x].astype(BF)
        down[a, :, x:] = (p31[a, :, x:] + wide(rm[a])).astype(BF)
        up[a, :, :z] = p11[a, :, :z].astype(BF)
        up[a, :, z:MID] = (p11[a, :, z:MID] + wide(rp[a, :, : MID - z])).astype(BF)
        up[a, :, MID:] = p20[a, :, MID:].astype(BF)
        flat[a, :, :MID] = p31[a, :, :MID].astype(BF)
        flat[a, :, MID:x] = (p11[a, :, MID:x] + wide(rp[a, :, MID - z :])).astype(BF)
        flat[a, :, x:] = p11[a, :, x:].astype(BF)


def scatter_far(p20, p11, p31, far_z, far_up, far_down):
    return pl.pallas_call(
        merge_kernel,
        out_shape=[jax.ShapeDtypeStruct((3, BLK, HALF), BF)] * 3,
        compiler_params=pltpu.CompilerParams(vmem_limit_bytes=32 << 20),
        cost_estimate=pl.CostEstimate(flops=0, bytes_accessed=6 << 20, transcendentals=0),
    )(p20, p11, p31, send(far_z, ZS), send(far_up, XP), send(far_down, XM))


def scatter_mid(down, up, flat, p10, p30, p01):
    rm, rp, rz = wide(send(down, XM)), wide(send(up, XP)), wide(send(flat, ZS))
    p10 = join(lo(p10), hi(p10) + hi(rp) + hi(rz))
    p30 = join(lo(p30) + lo(rm) + lo(rz), hi(p30))
    p01 = join(lo(p01) + lo(rp), hi(p01) + hi(rm))
    return p10.astype(BF), p30.astype(BF), p01.astype(BF)


def scatter_last(up, down, flat, p00):
    rp, rm, rz = send(up, XP), send(down, XM), send(flat, ZS)
    return p00 + wide(rp) + wide(rm) + wide(rz)


def rows(*blocks):
    return jnp.concatenate(blocks, axis=-2)


def after(*arrays):
    return lax.optimization_barrier(arrays)


def gather(e):
    z, x = CUTS
    g30, g10, g01 = send(e, XP), send(e, XM), send(e, ZS)
    rp = send(join(lo(g30), hi(g01)), XP)
    rm = send(join(lo(g01), hi(g10)), XM)
    rz = send(join(lo(g30), hi(g10)), ZS)
    rm, near = after(rm, rows(g10, g30, g01, e))
    turn_up = join(rz[..., z:MID], rp[..., MID:x])
    fz, fp, fm = send(rp[..., :z], ZS), send(turn_up, XP), send(rz[..., x:], XM)
    far, mids = after(join(fz, fp, fm), rows(rp, rm, rz))
    pieces = near, mids, far
    return pieces, [send(piece, CORE) for piece in pieces]


def local_grads(gate_sum, upper_sum, back_sum):
    sigmoid_gate = jax.nn.sigmoid(gate_sum)
    silu_gate = gate_sum * sigmoid_gate
    hidden = (silu_gate * upper_sum).astype(BF)
    grad_gate = (
        back_sum * upper_sum * sigmoid_gate * (1.0 + gate_sum * (1.0 - sigmoid_gate))
    ).astype(BF)
    grad_upper = (back_sum * silu_gate).astype(BF)
    return jnp.stack([grad_gate, grad_upper, hidden])


def shards(tokens, out_grad, gate_weight, up_weight, down_weight):
    gx = lax.axis_index("gx")
    core = gx % 2
    pos = jnp.stack([gx // 4, (gx // 2) % 2, core]).astype(jnp.int32)
    far_half = (1 - core) * HALF

    blocks = lax.all_to_all(spread(tokens, out_grad), "gy", 0, 0, tiled=True)
    weights = (gate_weight, up_weight, down_weight)
    weights_sib = [
        send(lax.dynamic_slice_in_dim(w, far_half, HALF, axis), CORE)
        for w, axis in zip(weights, (1, 1, 0))
    ]
    tg, tok_t = order(pos, blocks)
    tg_sib = send(tg, CORE)

    first = sums(pos, tg, tg_sib, weights, weights_sib, 0)
    p10, p30, p01, p00 = sums(pos, tg, tg_sib, weights, weights_sib, 1)
    mid = scatter_far(*first)
    last = scatter_mid(*mid, p10, p30, p01)
    total = scatter_last(*last, p00)
    own, sib = gather(local_grads(total[0], total[1], total[2]))

    gw, uw = gate_weight, up_weight
    terms, *grads = part(pos, own, 0, 0, (gw, uw, None), (tok_t, tg, None))
    terms, *grads = part(pos, own, 0, 1, (gw, uw, terms), (tok_t, tg, grads))
    (terms,) = part(pos, sib, 1, 0, (gw, uw, terms))
    (terms,) = part(pos, sib, 1, 1, (gw, uw, terms), None, True)
    grad_tokens = total_of(lax.all_to_all(terms, "gy", 0, 0, tiled=True))
    grads = part(pos, sib, 1, 0, None, (tok_t, tg, grads))
    ggw, guw, gdw = part(pos, sib, 1, 1, None, (tok_t, tg, grads))
    return grad_tokens, ggw, guw, gdw


def solution(mesh):
    return jax.shard_map(
        shards,
        mesh=mesh,
        in_specs=(P("gy", "gx"), P("gy", "gx"), P("gx", "gy"), P("gx", "gy"), P("gy", "gx")),
        out_specs=(P("gy", "gx"), P("gx", "gy"), P("gx", "gy"), P("gy", "gx")),
        check_vma=False,
    )
```
